128 devices in a mesh: blk: 16 (over x, z_lo, core), maps: 8 (over y, z_hi).
Axes of the slice: x: 4, y: 4, z: 4 (z_hi: 2, z_lo: 2; z = z_hi * 2 + z_lo), core: 2. Of those that a mesh axis runs over, the one named last changes fastest.
Arguments:
- inv_cov: float32 [24576, 24576], P('blk', 'maps'), as said below
- sim_maps: float32 [24576, 512], P(('maps', 'blk')), may hold values from -6 to 6
- templates: float32 [24576, 4608], P(('blk', 'maps')), may hold values from -0.009765625 to 0.009765625
- band_index: int32 [4608], P(('blk', 'maps')), may hold values from 0 to 47, as said below
Outputs:
- band_power: float32 [48, 512], replicated
- fisher_part: float32 [48, 48], replicated
The draws below stay inside these ranges and needn't reach their ends.
Inputs may be any that keep to these rules, and one draw needn't show every extreme that they name: `band_index`: every band holds at least 48 columns. `inv_cov`: Symmetric.
All inputs are finite; a program needn't handle non-finite values.
Results may differ from the reference program's by a relative error of at most 0.00016.
Values sent between devices are 32-bit elements; how exact they have to be, the bound alone decides.
No kernel may reach another device: no remote copies, remote signals or barrier semaphores. Data moves between devices by JAX's collectives and lax.ppermute only.
A program may use at most 128 MiB of HBM per device.

```python
import jax
import jax.numpy as jnp
from jax import lax

NPIX = 24576
NMODES = 4608
NBANDS = 48
NMAPS = 512


def draw_inv_cov(key, part):
    key = jax.random.fold_in(key, 3)
    key_entries, key_scale, key_diag = jax.random.split(key, 3)
    entries = jax.random.normal(key_entries, (NPIX, NPIX), jnp.float32)
    scales = jnp.exp(jax.random.uniform(key_scale, (NPIX,), jnp.float32, jnp.log(0.3), jnp.log(3.0)))
    symmetric = (entries + entries.T) * (0.70710678 / jnp.sqrt(jnp.float32(NPIX)))
    diag_vals = jnp.exp(jax.random.uniform(key_diag, (NPIX,), jnp.float32, jnp.log(0.5), jnp.log(2.0)))
    matrix = symmetric * scales[:, None] * scales[None, :]
    return matrix + jnp.diag(diag_vals * scales * scales)


def draw_band_index(key, part):
    key = jax.random.fold_in(key, 7)
    key_rand, key_perm = jax.random.split(key)
    half_len = NMODES // 2
    regular = jnp.arange(half_len, dtype=jnp.int32) % NBANDS
    random_part = jax.random.randint(key_rand, (half_len,), 0, NBANDS, dtype=jnp.int32)
    joined = jnp.concatenate([regular, random_part])
    return jax.random.permutation(key_perm, joined)


def level_of(rng, shape, cuts, least, top_value):
    def one(position, shards_of):
        steps = jax.random.uniform(jax.random.fold_in(jax.random.fold_in(rng, 6), position), (shards_of,), jnp.float32, least / len(cuts), top_value / len(cuts))
        return jnp.repeat(jnp.exp(steps), shape[position] // shards_of).reshape((-1,) + (1,) * (len(shape) - position - 1))

    factor_of = one(*cuts[0])
    for cut in cuts[1:]:
        factor_of = factor_of * one(*cut)
    return factor_of


def scatter_about(own_key, shape, spread, reach, pieces=(), kind=jnp.bfloat16):
    factor_of = level_of(own_key, shape, pieces, -0.22, 0.18) if pieces else 1.0
    array = jax.random.normal(own_key, shape, jnp.float32) * spread * factor_of
    return jnp.minimum(jnp.maximum(array, -reach), reach).astype(kind)


def setup_inputs(seed: int = 0) -> dict:
    arg_keys = jax.random.split(jax.random.key(seed), 5)
    return {
        "inv_cov": draw_inv_cov(jax.random.fold_in(arg_keys[4], 71), 0),
        "sim_maps": scatter_about(arg_keys[1], (NPIX, NMAPS), 1.0, 6.0, ((0, 128),), jnp.float32),
        "templates": scatter_about(arg_keys[2], (NPIX, NMODES), (16 * NPIX) ** -0.5, 0.009765625, ((0, 128),), jnp.float32),
        "band_index": draw_band_index(jax.random.fold_in(arg_keys[4], 71), 0),
    }


def reference(inv_cov, sim_maps, templates, band_index):
    high = lax.Precision.HIGHEST
    weighted = jnp.dot(inv_cov, sim_maps, precision=high, preferred_element_type=jnp.float32)
    modes = lax.dot_general(templates, weighted, (((0,), (0,)), ((), ())), precision=high, preferred_element_type=jnp.float32)
    onehot = (band_index[:, None] == jnp.arange(NBANDS, dtype=jnp.int32)[None, :]).astype(jnp.float32)
    band_sum = lax.dot_general(onehot, modes * modes, (((0,), (0,)), ((), ())), precision=high, preferred_element_type=jnp.float32)
    count = jnp.sum(onehot, axis=0)
    band_power = band_sum / (2.0 * count[:, None])
    centered = band_power - jnp.mean(band_power, axis=1, keepdims=True)
    fisher_part = jnp.dot(centered, centered.T, precision=high, preferred_element_type=jnp.float32) * ((NMODES / NBANDS) / NMAPS)
    return band_power, fisher_part
```

```python
import jax
import jax.numpy as jnp
from jax import lax
from jax.sharding import Mesh, PartitionSpec as P

NMODES = 4608
NBANDS = 48
NMAPS = 512
NY = 4
SPAN = NMODES // NY
HALF = NMAPS // 2
CHIPS = ("x", "zh", "zl")
EVERY = ("x", "zl", "c", "y", "zh")


def per_device(inv_cov, sim_maps, templates, band_index):
    high = lax.Precision.HIGH
    highest = lax.Precision.HIGHEST
    y = lax.axis_index("y")
    c = lax.axis_index("c")

    gathered = lax.all_gather(sim_maps, ("x", "zl", "c"), axis=0, tiled=True)

    spans = jnp.stack([templates[:, i * SPAN : (i + 1) * SPAN] for i in range(NY)])
    own = lax.all_to_all(spans, "y", 0, 0, tiled=True)
    other = lax.ppermute(own, "c", [(0, 1), (1, 0)])
    spread = jnp.stack([own, other], axis=1).reshape(1536, SPAN)

    bands = lax.all_to_all(
        jnp.broadcast_to(band_index[None, None, :], (128, 1, 36)), EVERY, 0, 0, tiled=True
    ).reshape(NMODES)

    partial = jnp.dot(inv_cov, gathered, precision=high, preferred_element_type=jnp.float32)
    partial = partial.reshape(8, 192, 2, HALF).transpose(2, 0, 1, 3).reshape(16, 192, HALF)
    partial, spread, bands = lax.optimization_barrier((partial, spread, bands))
    terms = lax.all_to_all(partial, ("c", "y", "zh"), 0, 0, tiled=True)
    rows = jnp.sum(terms.reshape(2, 8, 192, HALF), axis=1)
    rows = jnp.stack([rows[c], rows[1 - c]])
    weighted = lax.all_to_all(
        jnp.broadcast_to(rows[None], (NY, 2, 192, HALF)), "y", 0, 0, tiled=True
    ).reshape(1536, HALF)

    projected = lax.dot_general(
        weighted,
        spread,
        (((0,), (0,)), ((), ())),
        precision=high,
        preferred_element_type=jnp.float32,
    )
    pieces = lax.all_to_all(projected.reshape(16, 16, SPAN), CHIPS, 0, 0, tiled=True)
    modes = jnp.sum(pieces, axis=0)

    labels = jnp.arange(NBANDS, dtype=jnp.int32)
    count = jnp.sum((bands[None, :] == labels[:, None]).astype(jnp.float32), axis=1)
    mine = lax.dynamic_slice(bands, (y * SPAN,), (SPAN,))
    onehot = (mine[:, None] == labels[None, :]).astype(jnp.float32)
    sums = jnp.dot(modes * modes, onehot, precision=highest, preferred_element_type=jnp.float32)
    blocks = lax.all_to_all(
        jnp.broadcast_to(sums[None], (128, 16, NBANDS)), ("c",) + CHIPS + ("y",), 0, 0, tiled=True
    )
    band_sum = jnp.sum(blocks.reshape(32, NY, 16, NBANDS), axis=1).reshape(NMAPS, NBANDS).T
    band_power = band_sum / (2.0 * count[:, None])
    centered = band_power - jnp.mean(band_power, axis=1, keepdims=True)
    fisher_part = jnp.dot(
        centered, centered.T, precision=highest, preferred_element_type=jnp.float32
    ) * (NMODES / NBANDS / NMAPS)
    return (band_power, fisher_part)


def solution(mesh):
    split = Mesh(mesh.devices.reshape(4, 2, 2, 4, 2), EVERY)
    blk, maps = ("x", "zl", "c"), ("y", "zh")
    placed = (
        P(blk, maps),
        P(maps + blk, None),
        P(blk + maps, None),
        P(blk + maps),
    )
    return jax.shard_map(
        per_device, mesh=split, in_specs=placed, out_specs=(P(), P()), check_vma=False
    )
```

```python
import jax
import jax.numpy as jnp
from jax import lax
from jax.experimental import pallas as pl
from jax.experimental.pallas import tpu as pltpu
from jax.sharding import Mesh, PartitionSpec as P

NMODES = 4608
NBANDS = 48
NMAPS = 512
NY = 4
SPAN = NMODES // NY
HALF = NMAPS // 2
ROWS = 192
BLK = ("x", "zl", "c")
RING = ("y", "zh")
CHIPS = ("x", "zh", "zl")
EVERY = BLK + RING
MIB = 2**20
F32 = jnp.float32
BF16 = jnp.bfloat16


def split(value):
    high = value.astype(BF16)
    return high, (value - high.astype(F32)).astype(BF16)


def dot(a, b):
    return jnp.dot(a, b, preferred_element_type=F32)


def limit(mib):
    return pltpu.CompilerParams(vmem_limit_bytes=mib * MIB)


def shift(value, dy, dz):
    pairs = [
        (y * 2 + z, ((y + dy) % NY) * 2 + (z + dz) % 2)
        for y in range(NY)
        for z in range(2)
    ]
    return lax.ppermute(value, RING, pairs)


def swap(value):
    return lax.ppermute(value, "c", [(0, 1), (1, 0)])


def split_body(a, high, low):
    high[...], low[...] = split(a[...])


def split_rows(a):
    rows, cols = a.shape
    step = 128
    block = pl.BlockSpec((step, cols), lambda i: (i, 0))
    return pl.pallas_call(
        split_body,
        grid=(rows // step,),
        in_specs=[block],
        out_specs=[block] * 2,
        out_shape=[jax.ShapeDtypeStruct(a.shape, BF16)] * 2,
        compiler_params=limit(58),
        cost_estimate=pl.CostEstimate(
            flops=2 * rows * cols, bytes_accessed=8 * rows * cols, transcendentals=0
        ),
    )(a)


def add_step(out, value):
    @pl.when(pl.program_id(0) == 0)
    def _():
        out[...] = value

    @pl.when(pl.program_id(0) > 0)
    def _():
        out[...] += value


def first_body(at, a_high, a_low, s, out, s_high, s_low):
    sh, sl = split(s[...])
    s_high[...] = sh
    s_low[...] = sl
    ah = a_high[...]
    add_step(out, dot(ah, sh) + dot(ah, sl) + dot(a_low[...], sh))


def next_body(at, a_high, a_low, s_high, s_low, out):
    ah = a_high[...]
    sh = s_high[...]
    add_step(out, dot(ah, sh) + dot(ah, s_low[...]) + dot(a_low[...], sh))


def rows_of(at, a_high, a_low, maps):
    inner, cols = maps[0].shape
    step = 1024
    tall = 2 * ROWS
    a_block = pl.BlockSpec((tall, step), lambda k, at: (at[0], k))
    s_block = pl.BlockSpec((step, cols), lambda k, at: (k, 0))
    o_block = pl.BlockSpec((tall, cols), lambda k, at: (0, 0))
    o_shape = jax.ShapeDtypeStruct((tall, cols), F32)
    parts = jax.ShapeDtypeStruct((inner, cols), BF16)
    first = len(maps) == 1
    return pl.pallas_call(
        first_body if first else next_body,
        grid_spec=pltpu.PrefetchScalarGridSpec(
            num_scalar_prefetch=1,
            grid=(inner // step,),
            in_specs=[a_block, a_block] + [s_block] * len(maps),
            out_specs=[o_block, s_block, s_block] if first else o_block,
        ),
        out_shape=[o_shape, parts, parts] if first else o_shape,
        compiler_params=limit(58),
        cost_estimate=pl.CostEstimate(
            flops=6 * tall * inner * cols,
            bytes_accessed=4 * inner * (tall + cols),
            transcendentals=0,
        ),
    )(jnp.reshape(at, (1,)).astype(jnp.int32), a_high, a_low, *maps)


def project_body(terms, begun, *refs):
    out = refs[-1]
    cols = 384
    left = []
    for t in range(terms):
        w = refs[3 * t]
        wh, wl = split(jnp.concatenate([w[0], w[1]], axis=0).T)
        left.append(jnp.concatenate([wh, wh, wl], axis=1))
    for n in range(0, SPAN, cols):
        total = None
        for t in range(terms):
            own, other = refs[3 * t + 1 : 3 * t + 3]
            th, tl = split(
                jnp.concatenate([own[:, n : n + cols], other[:, n : n + cols]], axis=0)
            )
            term = dot(left[t], jnp.concatenate([th, tl, th], axis=0))
            total = term if total is None else total + term
        for half in range(2):
            part = total[128 * half : 128 * half + 128].reshape(16, 8, cols)
            if begun:
                part += refs[3 * terms][:, half, :, n : n + cols]
            out[:, half, :, n : n + cols] = part


def project(groups, begun=None):
    operands = [v for g in groups for v in g] + ([] if begun is None else [begun])

    def body(*refs):
        project_body(len(groups), begun is not None, *refs)

    return pl.pallas_call(
        body,
        out_shape=jax.ShapeDtypeStruct((16, 2, 8, SPAN), F32),
        compiler_params=limit(32),
        cost_estimate=pl.CostEstimate(
            flops=len(groups) * 6 * 2 * ROWS * HALF * SPAN,
            bytes_accessed=4 * sum(v.size for v in operands),
            transcendentals=0,
        ),
    )(*operands)


def band_body(pieces, onehot, out):
    modes = jnp.sum(pieces[...], axis=0)
    squares = modes * modes
    sums = jnp.dot(
        squares.reshape(16, SPAN),
        onehot[...],
        precision=lax.Precision.HIGHEST,
        preferred_element_type=F32,
    )
    lane = lax.broadcasted_iota(jnp.int32, (8, 128), 1)
    both = jnp.where(lane < NBANDS, sums[:8], sums[8:])
    out[...] = jnp.broadcast_to(both[None], out.shape)


def final_body(blocks, count, power, fisher):
    total = jnp.sum(blocks[...].reshape(32, NY, 8, 128), axis=1).reshape(HALF, 128).T
    scale = 2.0 * count[...]
    for c in range(2):
        for half in range(2):
            at = HALF * c + 128 * half
            power[:, at : at + 128] = (
                total[NBANDS * half : NBANDS * half + NBANDS, 128 * c : 128 * c + 128] / scale
            )
    value = power[...]
    centered = value - jnp.mean(value, axis=1, keepdims=True)
    fisher[...] = lax.dot_general(
        centered,
        centered,
        (((1,), (1,)), ((), ())),
        precision=lax.Precision.HIGHEST,
        preferred_element_type=F32,
    ) * (NMODES / NBANDS / NMAPS)


def per_device(inv_cov, sim_maps, templates, band_index):
    y = lax.axis_index("y")
    zh = lax.axis_index("zh")
    c = lax.axis_index("c")

    gathered = lax.all_gather(sim_maps, BLK, axis=0, tiled=True)

    own = []
    for dy in range(NY):
        block = lax.dynamic_slice(templates, (0, lax.rem(y + dy, NY) * SPAN), (ROWS, SPAN))
        own.append(shift(block, dy, 0) if dy else block)

    bands = lax.all_to_all(
        jnp.broadcast_to(band_index[None, None, :], (128, 1, 36)), EVERY, 0, 0, tiled=True
    )
    a_high, a_low = split_rows(inv_cov)
    gathered, a_high, a_low, bands, *own = lax.optimization_barrier(
        (gathered, a_high, a_low, bands, *own)
    )

    maps = (gathered,)
    sent = []
    for dy in (2, 1, 3, 0):
        found = rows_of(lax.rem(y + dy, NY), a_high, a_low, maps)
        if len(maps) == 1:
            found, *maps = found
        far = lax.dynamic_slice(found, ((1 - zh) * ROWS, 0), (ROWS, NMAPS))
        near = lax.dynamic_slice(found, (zh * ROWS, 0), (ROWS, NMAPS))
        sent.append(shift(far, dy, 1))
        sent.append(shift(near, dy, 0) if dy else near)

    bands = bands.reshape(NMODES)
    labels = jnp.arange(NBANDS, dtype=jnp.int32)
    count = jnp.sum((bands[None, :] == labels[:, None]).astype(F32), axis=1, keepdims=True)
    mine = lax.dynamic_slice(bands, (y * SPAN,), (SPAN,))
    lane = jnp.arange(128, dtype=jnp.int32)
    names = jnp.where(lane < 2 * NBANDS, lane % NBANDS, -1)
    onehot = (mine[:, None] == names[None, :]).astype(F32)

    rows = sent[0]
    for value in sent[1:]:
        rows = rows + value
    rows, count, onehot, *own = lax.optimization_barrier((rows, count, onehot, *own))

    keep = lax.dynamic_slice(rows, (0, c * HALF), (ROWS, HALF))
    give = lax.dynamic_slice(rows, (0, (1 - c) * HALF), (ROWS, HALF))
    pair = jnp.stack([keep, swap(give)])
    around = [shift(pair, dy, 0) if dy else pair for dy in range(NY)]
    other = [swap(v) for v in own]
    projected = project([(around[0], own[0], other[0])])
    projected = project([(around[d], own[d], other[d]) for d in (1, 3)], projected)
    projected = project([(around[2], own[2], other[2])], projected)

    pieces = lax.all_to_all(projected, CHIPS, 0, 0, tiled=True)
    sums = pl.pallas_call(
        band_body,
        out_shape=jax.ShapeDtypeStruct((128, 8, 128), F32),
        compiler_params=limit(32),
    )(pieces, onehot)
    blocks = lax.all_to_all(sums, ("c",) + CHIPS + ("y",), 0, 0, tiled=True)
    return pl.pallas_call(
        final_body,
        out_shape=[
            jax.ShapeDtypeStruct((NBANDS, NMAPS), F32),
            jax.ShapeDtypeStruct((NBANDS, NBANDS), F32),
        ],
        compiler_params=limit(32),
    )(blocks, count)


def solution(mesh):
    parts = Mesh(mesh.devices.reshape(4, 2, 2, 4, 2), EVERY)
    placed = (P(BLK, RING), P(RING + BLK, None), P(BLK + RING, None), P(BLK + RING))
    body = jax.shard_map(
        per_device, mesh=parts, in_specs=placed, out_specs=(P(), P()), check_vma=False
    )
    return lambda *arrays: tuple(body(*arrays))
```

```python
import jax
import jax.numpy as jnp
from jax import lax
from jax.experimental import pallas as pl
from jax.experimental.pallas import tpu as pltpu
from jax.sharding import Mesh, PartitionSpec as P

NMODES = 4608
NBANDS = 48
NMAPS = 512
NY = 4
SPAN = NMODES // NY
HALF = NMAPS // 2
ROWS = 192
BLK = ("x", "zl", "c")
RING = ("y", "zh")
CHIPS = ("x", "zh", "zl")
EVERY = BLK + RING
MIB = 2**20
F32 = jnp.float32
BF16 = jnp.bfloat16


def split(value):
    high = value.astype(BF16)
    return high, (value - high.astype(F32)).astype(BF16)


def dot(a, b):
    return jnp.dot(a, b, preferred_element_type=F32)


def limit(mib):
    return pltpu.CompilerParams(vmem_limit_bytes=mib * MIB)


def shift(value, dy, dz):
    pairs = [
        (y * 2 + z, ((y + dy) % NY) * 2 + (z + dz) % 2)
        for y in range(NY)
        for z in range(2)
    ]
    return lax.ppermute(value, RING, pairs)


def swap(value):
    return lax.ppermute(value, "c", [(0, 1), (1, 0)])


def split_body(a, high, low):
    high[...], low[...] = split(a[...])


def split_rows(a):
    rows, cols = a.shape
    step = 128
    block = pl.BlockSpec((step, cols), lambda i: (i, 0))
    return pl.pallas_call(
        split_body,
        grid=(rows // step,),
        in_specs=[block],
        out_specs=[block] * 2,
        out_shape=[jax.ShapeDtypeStruct(a.shape, BF16)] * 2,
        compiler_params=limit(32),
        cost_estimate=pl.CostEstimate(
            flops=2 * rows * cols, bytes_accessed=8 * rows * cols, transcendentals=0
        ),
    )(a)


def add_step(out, value):
    @pl.when(pl.program_id(0) == 0)
    def _():
        out[...] = value

    @pl.when(pl.program_id(0) > 0)
    def _():
        out[...] += value


def row_body(blocks, first, at, *refs):
    highs, lows, rest = refs[:blocks], refs[blocks : 2 * blocks], refs[2 * blocks :]
    if first:
        sh, sl = split(rest[0][...])
        rest[-2][...] = sh
        rest[-1][...] = sl
        outs = rest[1:-2]
    else:
        sh, sl = rest[0][...], rest[1][...]
        outs = rest[2:]
    ah = jnp.concatenate([ref[...] for ref in highs], axis=0)
    al = jnp.concatenate([ref[...] for ref in lows], axis=0)
    found = dot(ah, sh) + dot(ah, sl) + dot(al, sh)
    for n, out in enumerate(outs):
        add_step(out, found[n * ROWS : n * ROWS + ROWS])


def rows_of(at, a_high, a_low, maps):
    inner, cols = maps[0].shape
    step = 1024
    blocks, first = len(at), len(maps) == 1
    a_blocks = [pl.BlockSpec((ROWS, step), lambda k, at, n=n: (at[n], k)) for n in range(blocks)]
    s_block = pl.BlockSpec((step, cols), lambda k, at: (k, 0))
    o_block = pl.BlockSpec((ROWS, cols), lambda k, at: (0, 0))
    parts = [jax.ShapeDtypeStruct((inner, cols), BF16)] * 2 if first else []

    def body(*refs):
        row_body(blocks, first, *refs)

    found = pl.pallas_call(
        body,
        grid_spec=pltpu.PrefetchScalarGridSpec(
            num_scalar_prefetch=1,
            grid=(inner // step,),
            in_specs=a_blocks * 2 + [s_block] * len(maps),
            out_specs=[o_block] * blocks + [s_block] * len(parts),
        ),
        out_shape=[jax.ShapeDtypeStruct((ROWS, cols), F32)] * blocks + parts,
        compiler_params=limit(32),
        cost_estimate=pl.CostEstimate(
            flops=blocks * ROWS * cols,
            bytes_accessed=blocks * ROWS * cols,
            transcendentals=0,
        ),
    )(jnp.stack(at).astype(jnp.int32), *[a_high] * blocks, *[a_low] * blocks, *maps)
    return found[:blocks], found[blocks:] or maps


def project_body(terms, begun, *refs):
    out = refs[-1]
    cols = 384
    left = []
    for t in range(terms):
        w = refs[3 * t]
        wh, wl = split(jnp.concatenate([w[0], w[1]], axis=0).T)
        left.append(jnp.concatenate([wh, wh, wl], axis=1))
    for n in range(0, SPAN, cols):
        total = None
        for t in range(terms):
            own, other = refs[3 * t + 1 : 3 * t + 3]
            th, tl = split(
                jnp.concatenate([own[:, n : n + cols], other[:, n : n + cols]], axis=0)
            )
            term = dot(left[t], jnp.concatenate([th, tl, th], axis=0))
            total = term if total is None else total + term
        for half in range(2):
            part = total[128 * half : 128 * half + 128].reshape(16, 8, cols)
            if begun:
                part += refs[3 * terms][:, half, :, n : n + cols]
            out[:, half, :, n : n + cols] = part


def project(groups, begun=None):
    operands = [v for g in groups for v in g] + ([] if begun is None else [begun])

    def body(*refs):
        project_body(len(groups), begun is not None, *refs)

    return pl.pallas_call(
        body,
        out_shape=jax.ShapeDtypeStruct((16, 2, 8, SPAN), F32),
        compiler_params=limit(32),
        cost_estimate=pl.CostEstimate(
            flops=len(groups) * 6 * 2 * ROWS * HALF * SPAN,
            bytes_accessed=4 * sum(v.size for v in operands),
            transcendentals=0,
        ),
    )(*operands)


def names_row():
    lane = lax.broadcasted_iota(jnp.int32, (1, 128), 1)
    return jnp.where(
        lane < NBANDS, lane, jnp.where(lane < 2 * NBANDS, lane - NBANDS, -1)
    ).astype(F32)


def band_body(y, pieces, bands, out):
    devices, each = SPAN // 36, 36
    held = bands[pl.ds(y[0] * devices, devices)].reshape(devices, each).astype(F32)
    row = lax.broadcasted_iota(jnp.int32, (SPAN, devices), 0)
    begin = lax.broadcasted_iota(jnp.int32, (SPAN, devices), 1) * each
    source = ((row >= begin) & (row < begin + each)).astype(F32)
    start = jnp.sum(source * begin.astype(F32), axis=1, keepdims=True)
    at = lax.broadcasted_iota(jnp.int32, (SPAN, each), 0).astype(F32) - start
    mask = at == lax.broadcasted_iota(jnp.int32, (SPAN, each), 1).astype(F32)
    spread = jnp.dot(source, held, preferred_element_type=F32)
    band = jnp.sum(jnp.where(mask, spread, 0.0), axis=1, keepdims=True)
    onehot = (band == names_row()).astype(F32)

    modes = jnp.sum(pieces[...], axis=0)
    sums = jnp.dot(
        (modes * modes).reshape(16, SPAN),
        onehot,
        precision=lax.Precision.HIGHEST,
        preferred_element_type=F32,
    )
    lane = lax.broadcasted_iota(jnp.int32, (8, 128), 1)
    both = jnp.where(lane < NBANDS, sums[:8], sums[8:])
    out[...] = jnp.broadcast_to(both[None], out.shape)


def final_body(blocks, bands, power, fisher):
    held = bands[...].reshape(128, 36).astype(F32)
    names = names_row()
    found = jnp.zeros((128, 128), F32)
    for k in range(36):
        found += (held[:, k : k + 1] == names).astype(F32)
    count = jnp.maximum(jnp.sum(found, axis=0, keepdims=True), 1.0)
    total = jnp.sum(blocks[...].reshape(32, NY, 8, 128), axis=1).reshape(HALF, 128)
    total = (total / (2.0 * count)).T
    for c in range(2):
        for half in range(2):
            at = HALF * c + 128 * half
            power[:, at : at + 128] = total[
                NBANDS * half : NBANDS * half + NBANDS, 128 * c : 128 * c + 128
            ]
    value = power[...]
    centered = value - jnp.mean(value, axis=1, keepdims=True)
    fisher[...] = lax.dot_general(
        centered,
        centered,
        (((1,), (1,)), ((), ())),
        precision=lax.Precision.HIGHEST,
        preferred_element_type=F32,
    ) * (NMODES / NBANDS / NMAPS)


def per_device(inv_cov, sim_maps, templates, band_index):
    y = lax.axis_index("y")
    zh = lax.axis_index("zh")
    c = lax.axis_index("c")

    gathered = lax.all_gather(sim_maps, BLK, axis=0, tiled=True)

    own = []
    for dy in range(NY):
        block = lax.dynamic_slice(templates, (0, lax.rem(y + dy, NY) * SPAN), (ROWS, SPAN))
        own.append(shift(block, dy, 0) if dy else block)

    a_high, a_low = split_rows(inv_cov)
    gathered, a_high, a_low, *own = lax.optimization_barrier((gathered, a_high, a_low, *own))

    maps = [gathered]
    sent = []
    for group in (((2, 1), (2, 0)), ((1, 1), (1, 0)), ((3, 1), (3, 0)), ((0, 1),), ((0, 0),)):
        at = [lax.rem(y + dy, NY) * 2 + lax.rem(zh + dz, 2) for dy, dz in group]
        found, maps = rows_of(at, a_high, a_low, maps)
        found, maps = lax.optimization_barrier((found, maps))
        for (dy, dz), block in zip(group, found):
            sent.append(shift(block, dy, dz) if dy or dz else block)
    sent[-1], *own = lax.optimization_barrier((sent[-1], *own))
    other = [swap(v) for v in own]
    rows = sent[0]
    for value in sent[1:]:
        rows = rows + value
    rows, band_index, *other = lax.optimization_barrier((rows, band_index, *other))

    keep = lax.dynamic_slice(rows, (0, c * HALF), (ROWS, HALF))
    give = lax.dynamic_slice(rows, (0, (1 - c) * HALF), (ROWS, HALF))
    pair = jnp.stack([keep, swap(give)])
    around = [shift(pair, dy, 0) if dy else pair for dy in range(NY)]
    bands = lax.all_to_all(
        jnp.broadcast_to(band_index[None, None, :], (128, 1, 36)), EVERY, 0, 0, tiled=True
    )
    projected = project([(around[0], own[0], other[0])])
    projected = project([(around[d], own[d], other[d]) for d in (1, 3)], projected)
    projected = project([(around[2], own[2], other[2])], projected)

    projected, bands = lax.optimization_barrier((projected, bands))
    pieces = lax.all_to_all(projected, CHIPS, 0, 0, tiled=True)

    sums = pl.pallas_call(
        band_body,
        in_specs=[
            pl.BlockSpec(memory_space=pltpu.SMEM),
            pl.BlockSpec(memory_space=pltpu.VMEM),
            pl.BlockSpec(memory_space=pltpu.VMEM),
        ],
        out_shape=jax.ShapeDtypeStruct((128, 8, 128), F32),
        compiler_params=limit(32),
    )(jnp.reshape(y, (1,)).astype(jnp.int32), pieces, bands)
    blocks = lax.all_to_all(sums, ("c",) + CHIPS + ("y",), 0, 0, tiled=True)
    return pl.pallas_call(
        final_body,
        out_shape=[
            jax.ShapeDtypeStruct((NBANDS, NMAPS), F32),
            jax.ShapeDtypeStruct((NBANDS, NBANDS), F32),
        ],
        compiler_params=limit(32),
    )(blocks, bands)


def solution(mesh):
    parts = Mesh(mesh.devices.reshape(4, 2, 2, 4, 2), EVERY)
    placed = (P(BLK, RING), P(RING + BLK, None), P(BLK + RING, None), P(BLK + RING))
    body = jax.shard_map(
        per_device, mesh=parts, in_specs=placed, out_specs=(P(), P()), check_vma=False
    )
    return lambda *arrays: tuple(body(*arrays))
```

```python
import jax
import jax.numpy as jnp
from jax import lax
from jax.experimental import pallas as pl
from jax.experimental.pallas import tpu as pltpu
from jax.sharding import Mesh, PartitionSpec as P

NMODES = 4608
NBANDS = 48
NMAPS = 512
NY = 4
SPAN = NMODES // NY
HALF = NMAPS // 2
ROWS = 192
BLK = ("x", "zl", "c")
RING = ("y", "zh")
CHIPS = ("x", "zh", "zl")
EVERY = BLK + RING
MIB = 2**20
F32 = jnp.float32
BF16 = jnp.bfloat16


def split(value):
    high = value.astype(BF16)
    return high, (value - high.astype(F32)).astype(BF16)


def dot(a, b):
    return jnp.dot(a, b, preferred_element_type=F32)


def limit(mib):
    return pltpu.CompilerParams(vmem_limit_bytes=mib * MIB)


def shift(value, dy, dz):
    pairs = [
        (y * 2 + z, ((y + dy) % NY) * 2 + (z + dz) % 2)
        for y in range(NY)
        for z in range(2)
    ]
    return lax.ppermute(value, RING, pairs)


def swap(value):
    return lax.ppermute(value, "c", [(0, 1), (1, 0)])


def split_body(a, high, low):
    high[...], low[...] = split(a[...])


def split_rows(a):
    rows, cols = a.shape
    step = 128
    block = pl.BlockSpec((step, cols), lambda i: (i, 0))
    return pl.pallas_call(
        split_body,
        grid=(rows // step,),
        in_specs=[block],
        out_specs=[block] * 2,
        out_shape=[jax.ShapeDtypeStruct(a.shape, BF16)] * 2,
        compiler_params=limit(58),
        cost_estimate=pl.CostEstimate(
            flops=2 * rows * cols, bytes_accessed=8 * rows * cols, transcendentals=0
        ),
    )(a)


def rows_body(a_high, a_low, s, out):
    sh, sl = split(s[...])
    ah = a_high[...]
    found = dot(ah, sh) + dot(ah, sl) + dot(a_low[...], sh)

    for core in range(2):
        part = found[:, HALF * core : HALF * core + HALF].reshape(8, ROWS, HALF)
        mine = pl.ds(8 * core, 8)

        @pl.when(pl.program_id(0) == 0)
        def _():
            out[mine] = part

        @pl.when(pl.program_id(0) > 0)
        def _():
            out[mine] += part


def rows_of(a_high, a_low, maps):
    tall, inner = a_high.shape
    step = 512
    a_block = pl.BlockSpec((tall, step), lambda k: (0, k))
    return pl.pallas_call(
        rows_body,
        grid=(inner // step,),
        in_specs=[a_block, a_block, pl.BlockSpec((step, NMAPS), lambda k: (k, 0))],
        out_specs=pl.BlockSpec((16, ROWS, HALF), lambda k: (0, 0, 0)),
        out_shape=jax.ShapeDtypeStruct((16, ROWS, HALF), F32),
        compiler_params=limit(58),
        cost_estimate=pl.CostEstimate(
            flops=tall * inner, bytes_accessed=tall * inner, transcendentals=0
        ),
    )(a_high, a_low, maps)


def project_body(terms, begun, *refs):
    out = refs[-1]
    cols = 384
    left = []
    for t in range(terms):
        w = refs[3 * t]
        wh, wl = split(jnp.concatenate([w[0], w[1]], axis=0).T)
        left.append(jnp.concatenate([wh, wh, wl], axis=1))
    for n in range(0, SPAN, cols):
        total = None
        for t in range(terms):
            one, two = refs[3 * t + 1 : 3 * t + 3]
            th, tl = split(
                jnp.concatenate([one[:, n : n + cols], two[:, n : n + cols]], axis=0)
            )
            term = dot(left[t], jnp.concatenate([th, tl, th], axis=0))
            total = term if total is None else total + term
        for half in range(2):
            part = total[128 * half : 128 * half + 128].reshape(16, 8, cols)
            if begun:
                part += refs[3 * terms][:, half, :, n : n + cols]
            out[:, half, :, n : n + cols] = part


def project(groups, begun=None):
    operands = [v for g in groups for v in g] + ([] if begun is None else [begun])

    def body(*refs):
        project_body(len(groups), begun is not None, *refs)

    return pl.pallas_call(
        body,
        out_shape=jax.ShapeDtypeStruct((16, 2, 8, SPAN), F32),
        compiler_params=limit(32),
        cost_estimate=pl.CostEstimate(
            flops=len(groups) * 6 * 2 * ROWS * HALF * SPAN,
            bytes_accessed=4 * sum(v.size for v in operands),
            transcendentals=0,
        ),
    )(*operands)


def band_body(pieces, onehot, out):
    modes = jnp.sum(pieces[...], axis=0)
    squares = modes * modes
    sums = jnp.dot(
        squares.reshape(16, SPAN),
        onehot[...],
        precision=lax.Precision.HIGHEST,
        preferred_element_type=F32,
    )
    lane = lax.broadcasted_iota(jnp.int32, (8, 128), 1)
    both = jnp.where(lane < NBANDS, sums[:8], sums[8:])
    out[...] = jnp.broadcast_to(both[None], out.shape)


def final_body(blocks, count, power, fisher):
    total = jnp.sum(blocks[...].reshape(32, NY, 8, 128), axis=1).reshape(HALF, 128).T
    scale = 2.0 * count[...]
    for c in range(2):
        for half in range(2):
            at = HALF * c + 128 * half
            power[:, at : at + 128] = (
                total[NBANDS * half : NBANDS * half + NBANDS, 128 * c : 128 * c + 128] / scale
            )
    value = power[...]
    centered = value - jnp.mean(value, axis=1, keepdims=True)
    fisher[...] = lax.dot_general(
        centered,
        centered,
        (((1,), (1,)), ((), ())),
        precision=lax.Precision.HIGHEST,
        preferred_element_type=F32,
    ) * (NMODES / NBANDS / NMAPS)


def per_device(inv_cov, sim_maps, templates, band_index):
    y = lax.axis_index("y")
    c = lax.axis_index("c")

    gathered = lax.all_gather(sim_maps, BLK, axis=0, tiled=True)

    bands = lax.all_to_all(
        jnp.broadcast_to(band_index[None, None, :], (128, 1, 36)), EVERY, 0, 0, tiled=True
    )
    bands, templates = lax.optimization_barrier((bands, templates))

    own = []
    for dy in range(NY):
        block = lax.dynamic_slice(templates, (0, lax.rem(y + dy, NY) * SPAN), (ROWS, SPAN))
        own.append(shift(block, dy, 0) if dy else block)

    a_high, a_low = split_rows(inv_cov)
    gathered, a_high, a_low = lax.optimization_barrier((gathered, a_high, a_low))
    partial = rows_of(a_high, a_low, gathered)
    partial, bands, *own = lax.optimization_barrier((partial, bands, *own))
    terms = lax.all_to_all(partial, ("c",) + RING, 0, 0, tiled=True)

    other = [swap(v) for v in own]
    spread = [
        (jnp.where(c == 0, a, b), jnp.where(c == 0, b, a)) for a, b in zip(own, other)
    ]

    bands = bands.reshape(NMODES)
    labels = jnp.arange(NBANDS, dtype=jnp.int32)
    count = jnp.sum((bands[None, :] == labels[:, None]).astype(F32), axis=1, keepdims=True)
    mine = lax.dynamic_slice(bands, (y * SPAN,), (SPAN,))
    lane = jnp.arange(128, dtype=jnp.int32)
    names = jnp.where(lane < 2 * NBANDS, lane % NBANDS, -1)
    onehot = (mine[:, None] == names[None, :]).astype(F32)
    terms, count, onehot, spread = lax.optimization_barrier((terms, count, onehot, spread))

    rows = jnp.sum(terms.reshape(2, 8, ROWS, HALF), axis=1)
    around = [shift(rows, dy, 0) if dy else rows for dy in range(NY)]
    projected = project([(around[0], *spread[0])])
    projected = project([(around[d], *spread[d]) for d in (1, 3)], projected)
    projected = project([(around[2], *spread[2])], projected)

    pieces = lax.all_to_all(projected, CHIPS, 0, 0, tiled=True)
    sums = pl.pallas_call(
        band_body,
        out_shape=jax.ShapeDtypeStruct((128, 8, 128), F32),
        compiler_params=limit(32),
    )(pieces, onehot)
    blocks = lax.all_to_all(sums, ("c",) + CHIPS + ("y",), 0, 0, tiled=True)
    return pl.pallas_call(
        final_body,
        out_shape=[
            jax.ShapeDtypeStruct((NBANDS, NMAPS), F32),
            jax.ShapeDtypeStruct((NBANDS, NBANDS), F32),
        ],
        compiler_params=limit(32),
    )(blocks, count)


def solution(mesh):
    parts = Mesh(mesh.devices.reshape(4, 2, 2, 4, 2), EVERY)
    placed = (P(BLK, RING), P(RING + BLK, None), P(BLK + RING, None), P(BLK + RING))
    body = jax.shard_map(
        per_device, mesh=parts, in_specs=placed, out_specs=(P(), P()), check_vma=False
    )
    return lambda *arrays: tuple(body(*arrays))
```

```python
import jax
import jax.numpy as jnp
from jax import lax
from jax.experimental import pallas as pl
from jax.experimental.pallas import tpu as pltpu
from jax.sharding import Mesh, PartitionSpec as P

NMODES = 4608
NBANDS = 48
NMAPS = 512
NX = 4
SPAN = NMODES // NX
HALF = NMAPS // 2
ROWS = 192
BLK = ("x", "zl", "c")
RING = ("y", "zh")
CHIPS = ("y", "zh", "zl")
EVERY = BLK + RING
MIB = 2**20
F32 = jnp.float32
BF16 = jnp.bfloat16


def split(value):
    high = value.astype(BF16)
    return high, (value - high.astype(F32)).astype(BF16)


def dot(a, b):
    return jnp.dot(a, b, preferred_element_type=F32)


def limit(mib):
    return pltpu.CompilerParams(vmem_limit_bytes=mib * MIB)


def shift(value, step):
    return lax.ppermute(value, "x", [(n, (n + step) % NX) for n in range(NX)])


def swap(value):
    return lax.ppermute(value, "c", [(0, 1), (1, 0)])


def split_body(a, high, low):
    for core in range(2):
        for n in range(4):
            at = 4 * n + core
            value = jnp.concatenate(
                [a[:, at * ROWS : (at + 1) * ROWS], a[:, (at + 2) * ROWS : (at + 3) * ROWS]],
                axis=1,
            )
            to = pl.ds((core * 4 + n) * 2 * ROWS, 2 * ROWS)
            high[:, to], low[:, to] = split(value)


def split_rows(a):
    rows, cols = a.shape
    step = 128
    block = pl.BlockSpec((step, cols), lambda i: (i, 0))
    return pl.pallas_call(
        split_body,
        grid=(rows // step,),
        in_specs=[block],
        out_specs=[block] * 2,
        out_shape=[jax.ShapeDtypeStruct(a.shape, BF16)] * 2,
        compiler_params=limit(58),
        cost_estimate=pl.CostEstimate(
            flops=2 * rows * cols, bytes_accessed=8 * rows * cols, transcendentals=0
        ),
    )(a)


def rows_body(begun, core, a_high, a_low, s, *refs):
    out = refs[-1]
    sh, sl = split(s[...])
    ah = a_high[...]
    found = dot(ah, sh) + dot(ah, sl) + dot(a_low[...], sh)

    for half in range(2):
        part = found[:, HALF * half : HALF * half + HALF].reshape(8, ROWS, HALF)
        mine = pl.ds(8 * half, 8)

        @pl.when(pl.program_id(0) == 0)
        def _():
            out[mine] = part + refs[0][mine] if begun else part

        @pl.when(pl.program_id(0) > 0)
        def _():
            out[mine] += part


def rows_of(core, a_high, a_low, maps, begun=None):
    tall, inner = a_high.shape[0], maps.shape[0]
    step = 512
    steps = inner // step
    a_block = pl.BlockSpec((tall, step), lambda k, core: (0, core[0] * steps + k))
    whole = pl.BlockSpec((16, ROWS, HALF), lambda k, core: (0, 0, 0))
    more = [] if begun is None else [begun]

    def body(*refs):
        rows_body(len(more), *refs)

    return pl.pallas_call(
        body,
        grid_spec=pltpu.PrefetchScalarGridSpec(
            num_scalar_prefetch=1,
            grid=(steps,),
            in_specs=[a_block, a_block, pl.BlockSpec((step, NMAPS), lambda k, core: (k, 0))]
            + [whole] * len(more),
            out_specs=whole,
        ),
        out_shape=jax.ShapeDtypeStruct((16, ROWS, HALF), F32),
        compiler_params=limit(58),
        cost_estimate=pl.CostEstimate(
            flops=tall * inner, bytes_accessed=tall * inner, transcendentals=0
        ),
    )(jnp.reshape(core, (1,)).astype(jnp.int32), a_high, a_low, maps, *more)


def project_body(terms, begun, *refs):
    out = refs[-1]
    cols = 384
    left = []
    for t in range(terms):
        w = refs[3 * t]
        wh, wl = split(jnp.concatenate([w[0], w[1]], axis=0).T)
        left.append(jnp.concatenate([wh, wh, wl], axis=1))
    for n in range(0, SPAN, cols):
        total = None
        for t in range(terms):
            one, two = refs[3 * t + 1 : 3 * t + 3]
            th, tl = split(
                jnp.concatenate([one[:, n : n + cols], two[:, n : n + cols]], axis=0)
            )
            term = dot(left[t], jnp.concatenate([th, tl, th], axis=0))
            total = term if total is None else total + term
        for half in range(2):
            part = total[128 * half : 128 * half + 128].reshape(16, 8, cols)
            if begun:
                part += refs[3 * terms][:, half, :, n : n + cols]
            out[:, half, :, n : n + cols] = part


def project(groups, begun=None):
    operands = [v for g in groups for v in g] + ([] if begun is None else [begun])

    def body(*refs):
        project_body(len(groups), begun is not None, *refs)

    return pl.pallas_call(
        body,
        out_shape=jax.ShapeDtypeStruct((16, 2, 8, SPAN), F32),
        compiler_params=limit(32),
        cost_estimate=pl.CostEstimate(
            flops=len(groups) * 6 * 2 * ROWS * HALF * SPAN,
            bytes_accessed=4 * sum(v.size for v in operands),
            transcendentals=0,
        ),
    )(*operands)


def names_row():
    lane = lax.broadcasted_iota(jnp.int32, (1, 128), 1)
    return jnp.where(
        lane < NBANDS, lane, jnp.where(lane < 2 * NBANDS, lane - NBANDS, -1)
    ).astype(F32)


def band_body(x, pieces, bands, out):
    devices, each = SPAN // 36, 36
    held = bands[pl.ds(x[0] * devices, devices)].reshape(devices, each).astype(F32)
    row = lax.broadcasted_iota(jnp.int32, (SPAN, devices), 0)
    begin = lax.broadcasted_iota(jnp.int32, (SPAN, devices), 1) * each
    source = ((row >= begin) & (row < begin + each)).astype(F32)
    start = jnp.sum(source * begin.astype(F32), axis=1, keepdims=True)
    at = lax.broadcasted_iota(jnp.int32, (SPAN, each), 0).astype(F32) - start
    mask = at == lax.broadcasted_iota(jnp.int32, (SPAN, each), 1).astype(F32)
    spread = jnp.dot(source, held, preferred_element_type=F32)
    band = jnp.sum(jnp.where(mask, spread, 0.0), axis=1, keepdims=True)
    onehot = (band == names_row()).astype(F32)

    modes = jnp.sum(pieces[...], axis=0)
    sums = jnp.dot(
        (modes * modes).reshape(16, SPAN),
        onehot,
        precision=lax.Precision.HIGHEST,
        preferred_element_type=F32,
    )
    lane = lax.broadcasted_iota(jnp.int32, (8, 128), 1)
    both = jnp.where(lane < NBANDS, sums[:8], sums[8:])
    out[...] = jnp.broadcast_to(both[None], out.shape)


def final_body(blocks, bands, power, fisher):
    held = bands[...].reshape(128, 36).astype(F32).T
    label = lax.broadcasted_iota(jnp.int32, (NBANDS, 128), 0).astype(F32)
    found = jnp.zeros((NBANDS, 128), F32)
    for n in range(36):
        found += (held[n : n + 1] == label).astype(F32)
    scale = 2.0 * jnp.sum(found, axis=1, keepdims=True)
    total = jnp.sum(blocks[...].reshape(32, NX, 8, 128), axis=1).reshape(HALF, 128).T
    for c in range(2):
        for half in range(2):
            at = HALF * c + 128 * half
            power[:, at : at + 128] = (
                total[NBANDS * half : NBANDS * half + NBANDS, 128 * c : 128 * c + 128] / scale
            )
    value = power[...]
    centered = value - jnp.mean(value, axis=1, keepdims=True)
    fisher[...] = lax.dot_general(
        centered,
        centered,
        (((1,), (1,)), ((), ())),
        precision=lax.Precision.HIGHEST,
        preferred_element_type=F32,
    ) * (NMODES / NBANDS / NMAPS)


def per_device(inv_cov, sim_maps, templates, band_index):
    x = lax.axis_index("x")
    c = lax.axis_index("c")

    here = lax.all_to_all(
        jnp.broadcast_to(sim_maps[None], (8, ROWS, NMAPS)), ("x", "zl"), 0, 0, tiled=True
    ).reshape(8 * ROWS, NMAPS)

    own = []
    for step in range(NX):
        block = lax.dynamic_slice(templates, (0, lax.rem(x + step, NX) * SPAN), (ROWS, SPAN))
        own.append(shift(block, step) if step else block)

    a_high, a_low = split_rows(inv_cov)
    here, a_high, a_low = lax.optimization_barrier((here, a_high, a_low))
    there = swap(here)
    partial = rows_of(c, a_high, a_low, here)
    partial = rows_of(1 - c, a_high, a_low, there, partial)
    terms = lax.all_to_all(partial, ("c",) + RING, 0, 0, tiled=True)

    other = [swap(v) for v in own]
    spread = [
        (jnp.where(c == 0, a, b), jnp.where(c == 0, b, a)) for a, b in zip(own, other)
    ]

    terms, band_index, spread = lax.optimization_barrier((terms, band_index, spread))

    rows = jnp.sum(terms.reshape(2, 8, ROWS, HALF), axis=1)
    around = [shift(rows, step) if step else rows for step in range(NX)]
    bands = lax.all_to_all(
        jnp.broadcast_to(band_index[None, None, :], (128, 1, 36)), EVERY, 0, 0, tiled=True
    )
    projected = project([(around[0], *spread[0])])
    projected = project([(around[d], *spread[d]) for d in (1, 3)], projected)
    projected = project([(around[2], *spread[2])], projected)

    projected, bands = lax.optimization_barrier((projected, bands))
    pieces = lax.all_to_all(projected, CHIPS, 0, 0, tiled=True)
    sums = pl.pallas_call(
        band_body,
        in_specs=[
            pl.BlockSpec(memory_space=pltpu.SMEM),
            pl.BlockSpec(memory_space=pltpu.VMEM),
            pl.BlockSpec(memory_space=pltpu.VMEM),
        ],
        out_shape=jax.ShapeDtypeStruct((128, 8, 128), F32),
        compiler_params=limit(32),
    )(jnp.reshape(x, (1,)).astype(jnp.int32), pieces, bands)
    blocks = lax.all_to_all(sums, ("c",) + CHIPS + ("x",), 0, 0, tiled=True)
    return pl.pallas_call(
        final_body,
        out_shape=[
            jax.ShapeDtypeStruct((NBANDS, NMAPS), F32),
            jax.ShapeDtypeStruct((NBANDS, NBANDS), F32),
        ],
        compiler_params=limit(32),
    )(blocks, bands)


def solution(mesh):
    parts = Mesh(mesh.devices.reshape(4, 2, 2, 4, 2), EVERY)
    placed = (P(BLK, RING), P(RING + BLK, None), P(BLK + RING, None), P(BLK + RING))
    body = jax.shard_map(
        per_device, mesh=parts, in_specs=placed, out_specs=(P(), P()), check_vma=False
    )
    return lambda *arrays: tuple(body(*arrays))
```

```python
import jax
import jax.numpy as jnp
from jax import lax
from jax.experimental import pallas as pl
from jax.experimental.pallas import tpu as pltpu
from jax.sharding import Mesh, PartitionSpec as P

NMODES = 4608
NBANDS = 48
NMAPS = 512
NY = 4
SPAN = NMODES // NY
HALF = NMAPS // 2
PART = HALF // 2
ROWS = 192
BLK = ("x", "zl", "c")
RING = ("y", "zh")
CHIPS = ("x", "zh", "zl")
EVERY = BLK + RING
MIB = 2**20
F32 = jnp.float32
BF16 = jnp.bfloat16


def split(value):
    high = value.astype(BF16)
    return high, (value - high.astype(F32)).astype(BF16)


def dot(a, b):
    return jnp.dot(a, b, preferred_element_type=F32)


def limit(mib):
    return pltpu.CompilerParams(vmem_limit_bytes=mib * MIB)


def shift(value, dy, dz):
    pairs = [
        (y * 2 + z, ((y + dy) % NY) * 2 + (z + dz) % 2)
        for y in range(NY)
        for z in range(2)
    ]
    return lax.ppermute(value, RING, pairs)


def swap(value):
    return lax.ppermute(value, "c", [(0, 1), (1, 0)])


def split_body(a, high, low):
    high[...], low[...] = split(a[...])


def split_rows(a):
    rows, cols = a.shape
    step = 128
    block = pl.BlockSpec((step, cols), lambda i: (i, 0))
    return pl.pallas_call(
        split_body,
        grid=(rows // step,),
        in_specs=[block],
        out_specs=[block] * 2,
        out_shape=[jax.ShapeDtypeStruct(a.shape, BF16)] * 2,
        compiler_params=limit(58),
        cost_estimate=pl.CostEstimate(
            flops=2 * rows * cols, bytes_accessed=8 * rows * cols, transcendentals=0
        ),
    )(a)


def rows_body(a_high, a_low, s0, s1, out):
    sh, sl = split(jnp.concatenate([s0[...], s1[...]], axis=1))
    ah = a_high[...]
    found = dot(ah, sh) + dot(ah, sl) + dot(a_low[...], sh)

    for core in range(2):
        part = found[:, PART * core : PART * core + PART].reshape(8, ROWS, PART)
        mine = pl.ds(8 * core, 8)

        @pl.when(pl.program_id(0) == 0)
        def _():
            out[mine] = part

        @pl.when(pl.program_id(0) > 0)
        def _():
            out[mine] += part


def rows_of(a_high, a_low, maps, half):
    tall, inner = a_high.shape
    step = 512
    a_block = pl.BlockSpec((tall, step), lambda k: (0, k))
    return pl.pallas_call(
        rows_body,
        grid=(inner // step,),
        in_specs=[
            a_block,
            a_block,
            pl.BlockSpec((step, PART), lambda k: (k, half)),
            pl.BlockSpec((step, PART), lambda k: (k, 2 + half)),
        ],
        out_specs=pl.BlockSpec((16, ROWS, PART), lambda k: (0, 0, 0)),
        out_shape=jax.ShapeDtypeStruct((16, ROWS, PART), F32),
        compiler_params=limit(58),
        cost_estimate=pl.CostEstimate(
            flops=tall * inner, bytes_accessed=tall * inner, transcendentals=0
        ),
    )(a_high, a_low, maps, maps)


def project_body(terms, begun, earlier, *refs):
    out = refs[-1]
    cols = 384
    left = []
    for t in range(terms):
        w = refs[3 * t]
        wh, wl = split(jnp.concatenate([w[0], w[1]], axis=0).T)
        left.append(jnp.concatenate([wh, wh, wl], axis=1))
    for n in range(0, SPAN, cols):
        total = None
        for t in range(terms):
            one, two = refs[3 * t + 1 : 3 * t + 3]
            th, tl = split(
                jnp.concatenate([one[:, n : n + cols], two[:, n : n + cols]], axis=0)
            )
            term = dot(left[t], jnp.concatenate([th, tl, th], axis=0))
            total = term if total is None else total + term
        part = total.reshape(16, 8, cols)
        if begun:
            part += refs[3 * terms][:, :, n : n + cols]
        if earlier:
            out[:, 0, :, n : n + cols] = refs[3 * terms + 1][:, :, n : n + cols]
            out[:, 1, :, n : n + cols] = part
        else:
            out[:, :, n : n + cols] = part


def project(groups, begun=None, earlier=None):
    more = [v for v in (begun, earlier) if v is not None]
    operands = [v for g in groups for v in g] + more

    def body(*refs):
        project_body(len(groups), begun is not None, earlier is not None, *refs)

    shape = (16, 8, SPAN) if earlier is None else (16, 2, 8, SPAN)
    return pl.pallas_call(
        body,
        out_shape=jax.ShapeDtypeStruct(shape, F32),
        compiler_params=limit(32),
        cost_estimate=pl.CostEstimate(
            flops=len(groups) * 6 * 2 * ROWS * PART * SPAN,
            bytes_accessed=4 * sum(v.size for v in operands),
            transcendentals=0,
        ),
    )(*operands)


def band_body(pieces, onehot, out):
    modes = jnp.sum(pieces[...], axis=0)
    squares = modes * modes
    sums = jnp.dot(
        squares.reshape(16, SPAN),
        onehot[...],
        precision=lax.Precision.HIGHEST,
        preferred_element_type=F32,
    )
    lane = lax.broadcasted_iota(jnp.int32, (8, 128), 1)
    both = jnp.where(lane < NBANDS, sums[:8], sums[8:])
    out[...] = jnp.broadcast_to(both[None], out.shape)


def final_body(blocks, count, power, fisher):
    total = jnp.sum(blocks[...].reshape(32, NY, 8, 128), axis=1).reshape(HALF, 128).T
    scale = 2.0 * count[...]
    for c in range(2):
        for half in range(2):
            at = HALF * c + 128 * half
            power[:, at : at + 128] = (
                total[NBANDS * half : NBANDS * half + NBANDS, 128 * c : 128 * c + 128] / scale
            )
    value = power[...]
    centered = value - jnp.mean(value, axis=1, keepdims=True)
    fisher[...] = lax.dot_general(
        centered,
        centered,
        (((1,), (1,)), ((), ())),
        precision=lax.Precision.HIGHEST,
        preferred_element_type=F32,
    ) * (NMODES / NBANDS / NMAPS)


def per_device(inv_cov, sim_maps, templates, band_index):
    y = lax.axis_index("y")
    c = lax.axis_index("c")

    gathered = lax.all_gather(sim_maps, BLK, axis=0, tiled=True)

    bands = lax.all_to_all(
        jnp.broadcast_to(band_index[None, None, :], (128, 1, 36)), EVERY, 0, 0, tiled=True
    )
    bands, templates = lax.optimization_barrier((bands, templates))

    own = []
    for dy in range(NY):
        block = lax.dynamic_slice(templates, (0, lax.rem(y + dy, NY) * SPAN), (ROWS, SPAN))
        own.append(shift(block, dy, 0) if dy else block)

    a_high, a_low = split_rows(inv_cov)
    gathered, a_high, a_low = lax.optimization_barrier((gathered, a_high, a_low))
    early = rows_of(a_high, a_low, gathered, 0)
    early, bands, *own = lax.optimization_barrier((early, bands, *own))
    early = lax.all_to_all(early, ("c",) + RING, 0, 0, tiled=True)
    late = rows_of(a_high, a_low, gathered, 1)

    other = [swap(v) for v in own]
    spread = [
        (jnp.where(c == 0, a, b), jnp.where(c == 0, b, a)) for a, b in zip(own, other)
    ]

    bands = bands.reshape(NMODES)
    labels = jnp.arange(NBANDS, dtype=jnp.int32)
    count = jnp.sum((bands[None, :] == labels[:, None]).astype(F32), axis=1, keepdims=True)
    mine = lax.dynamic_slice(bands, (y * SPAN,), (SPAN,))
    lane = jnp.arange(128, dtype=jnp.int32)
    names = jnp.where(lane < 2 * NBANDS, lane % NBANDS, -1)
    onehot = (mine[:, None] == names[None, :]).astype(F32)
    early, late, count, onehot, spread = lax.optimization_barrier(
        (early, late, count, onehot, spread)
    )
    late = lax.all_to_all(late, ("c",) + RING, 0, 0, tiled=True)

    def gather(terms):
        rows = jnp.sum(terms.reshape(2, 8, ROWS, PART), axis=1)
        return [shift(rows, dy, 0) if dy else rows for dy in range(NY)]

    first = project([(w, *t) for w, t in zip(gather(early), spread)])
    first, late = lax.optimization_barrier((first, late))
    around = gather(late)
    projected = project([(around[0], *spread[0])])
    projected = project([(around[d], *spread[d]) for d in (1, 3)], projected)
    projected = project([(around[2], *spread[2])], projected, first)

    pieces = lax.all_to_all(projected, CHIPS, 0, 0, tiled=True)
    sums = pl.pallas_call(
        band_body,
        out_shape=jax.ShapeDtypeStruct((128, 8, 128), F32),
        compiler_params=limit(32),
    )(pieces, onehot)
    blocks = lax.all_to_all(sums, ("c",) + CHIPS + ("y",), 0, 0, tiled=True)
    return pl.pallas_call(
        final_body,
        out_shape=[
            jax.ShapeDtypeStruct((NBANDS, NMAPS), F32),
            jax.ShapeDtypeStruct((NBANDS, NBANDS), F32),
        ],
        compiler_params=limit(32),
    )(blocks, count)


def solution(mesh):
    parts = Mesh(mesh.devices.reshape(4, 2, 2, 4, 2), EVERY)
    placed = (P(BLK, RING), P(RING + BLK, None), P(BLK + RING, None), P(BLK + RING))
    body = jax.shard_map(
        per_device, mesh=parts, in_specs=placed, out_specs=(P(), P()), check_vma=False
    )
    return lambda *arrays: tuple(body(*arrays))
```

```python
import jax
import jax.numpy as jnp
from jax import lax
from jax.experimental import pallas as pl
from jax.experimental.pallas import tpu as pltpu
from jax.sharding import Mesh, PartitionSpec as P

NMODES = 4608
NBANDS = 48
NMAPS = 512
NY = 4
SPAN = NMODES // NY
HALF = NMAPS // 2
ROWS = 192
BLK = ("x", "zl", "c")
RING = ("y", "zh")
CHIPS = ("x", "zh", "zl")
EVERY = BLK + RING
MIB = 2**20
F32 = jnp.float32
BF16 = jnp.bfloat16


def split(value):
    high = value.astype(BF16)
    return high, (value - high.astype(F32)).astype(BF16)


def dot(a, b):
    return jnp.dot(a, b, preferred_element_type=F32)


def limit(mib):
    return pltpu.CompilerParams(vmem_limit_bytes=mib * MIB)


def shift(value, dy, dz):
    pairs = [
        (y * 2 + z, ((y + dy) % NY) * 2 + (z + dz) % 2)
        for y in range(NY)
        for z in range(2)
    ]
    return lax.ppermute(value, RING, pairs)


def swap(value):
    return lax.ppermute(value, "c", [(0, 1), (1, 0)])


def split_body(a, high, low):
    high[...], low[...] = split(a[...])


def split_rows(a):
    rows, cols = a.shape
    step = 128
    block = pl.BlockSpec((step, cols), lambda i: (i, 0))
    return pl.pallas_call(
        split_body,
        grid=(rows // step,),
        in_specs=[block],
        out_specs=[block] * 2,
        out_shape=[jax.ShapeDtypeStruct(a.shape, BF16)] * 2,
        compiler_params=limit(58),
        cost_estimate=pl.CostEstimate(
            flops=2 * rows * cols, bytes_accessed=8 * rows * cols, transcendentals=0
        ),
    )(a)


def add_step(out, value):
    @pl.when(pl.program_id(0) == 0)
    def _():
        out[...] = value

    @pl.when(pl.program_id(0) > 0)
    def _():
        out[...] += value


def row_body(at, far_high, near_high, far_low, near_low, s, far, near):
    sh, sl = split(s[...])
    ah = jnp.concatenate([far_high[...], near_high[...]], axis=0)
    al = jnp.concatenate([far_low[...], near_low[...]], axis=0)
    found = dot(ah, sh) + dot(ah, sl) + dot(al, sh)
    add_step(far, found[:ROWS])
    add_step(near, found[ROWS:])


def rows_of(far, near, a_high, a_low, maps):
    inner, cols = maps.shape
    step = 1024
    a_blocks = [pl.BlockSpec((ROWS, step), lambda k, at, n=n: (at[n], k)) for n in range(2)]
    o_block = pl.BlockSpec((ROWS, cols), lambda k, at: (0, 0))
    return pl.pallas_call(
        row_body,
        grid_spec=pltpu.PrefetchScalarGridSpec(
            num_scalar_prefetch=1,
            grid=(inner // step,),
            in_specs=a_blocks * 2 + [pl.BlockSpec((step, cols), lambda k, at: (k, 0))],
            out_specs=[o_block] * 2,
        ),
        out_shape=[jax.ShapeDtypeStruct((ROWS, cols), F32)] * 2,
        compiler_params=limit(58),
        cost_estimate=pl.CostEstimate(
            flops=12 * ROWS * inner * cols,
            bytes_accessed=4 * inner * (2 * ROWS + cols),
            transcendentals=0,
        ),
    )(jnp.stack([far, near]).astype(jnp.int32), a_high, a_high, a_low, a_low, maps)


def project_body(terms, begun, at, *refs):
    out = refs[-1]
    cols = 384
    left = []
    for t in range(terms):
        w = refs[3 * t]
        wh, wl = split(jnp.concatenate([w[0], w[1]], axis=0).T)
        left.append(jnp.concatenate([wh, wh, wl], axis=1))
    for n in range(0, SPAN, cols):
        total = None
        for t in range(terms):
            own, other = refs[3 * t + 1 : 3 * t + 3]
            th, tl = split(
                jnp.concatenate([own[0, :, n : n + cols], other[0, :, n : n + cols]], axis=0)
            )
            term = dot(left[t], jnp.concatenate([th, tl, th], axis=0))
            total = term if total is None else total + term
        for half in range(2):
            part = total[128 * half : 128 * half + 128].reshape(16, 8, cols)
            if begun:
                part += refs[3 * terms][:, half, :, n : n + cols]
            out[:, half, :, n : n + cols] = part


def project(at, weighted, own, other, begun=None):
    terms = len(weighted)
    operands = [v for w in weighted for v in (w, own, other)]
    in_specs = []
    for t in range(terms):
        block = pl.BlockSpec((1, ROWS, SPAN), lambda i, at, t=t: (at[t], 0, 0))
        in_specs += [pl.BlockSpec((2, ROWS, HALF), lambda i, at: (0, 0, 0)), block, block]
    whole = pl.BlockSpec((16, 2, 8, SPAN), lambda i, at: (0, 0, 0, 0))
    if begun is not None:
        operands.append(begun)
        in_specs.append(whole)

    def body(*refs):
        project_body(terms, begun is not None, *refs)

    return pl.pallas_call(
        body,
        grid_spec=pltpu.PrefetchScalarGridSpec(
            num_scalar_prefetch=1, grid=(1,), in_specs=in_specs, out_specs=whole
        ),
        out_shape=jax.ShapeDtypeStruct((16, 2, 8, SPAN), F32),
        compiler_params=limit(32),
        cost_estimate=pl.CostEstimate(
            flops=terms * 6 * 2 * ROWS * HALF * SPAN,
            bytes_accessed=8 * terms * ROWS * SPAN,
            transcendentals=0,
        ),
    )(jnp.stack(at).astype(jnp.int32), *operands)


def names_row():
    lane = lax.broadcasted_iota(jnp.int32, (1, 128), 1)
    return jnp.where(
        lane < NBANDS, lane, jnp.where(lane < 2 * NBANDS, lane - NBANDS, -1)
    ).astype(F32)


def band_body(y, pieces, bands, out):
    devices, each = SPAN // 36, 36
    held = bands[pl.ds(y[0] * devices, devices)].reshape(devices, each).astype(F32)
    row = lax.broadcasted_iota(jnp.int32, (SPAN, devices), 0)
    begin = lax.broadcasted_iota(jnp.int32, (SPAN, devices), 1) * each
    source = ((row >= begin) & (row < begin + each)).astype(F32)
    start = jnp.sum(source * begin.astype(F32), axis=1, keepdims=True)
    at = lax.broadcasted_iota(jnp.int32, (SPAN, each), 0).astype(F32) - start
    mask = at == lax.broadcasted_iota(jnp.int32, (SPAN, each), 1).astype(F32)
    spread = jnp.dot(source, held, preferred_element_type=F32)
    band = jnp.sum(jnp.where(mask, spread, 0.0), axis=1, keepdims=True)
    onehot = (band == names_row()).astype(F32)

    modes = jnp.sum(pieces[...], axis=0)
    sums = jnp.dot(
        (modes * modes).reshape(16, SPAN),
        onehot,
        precision=lax.Precision.HIGHEST,
        preferred_element_type=F32,
    )
    lane = lax.broadcasted_iota(jnp.int32, (8, 128), 1)
    both = jnp.where(lane < NBANDS, sums[:8], sums[8:])
    out[...] = jnp.broadcast_to(both[None], out.shape)


def final_body(blocks, bands, power, fisher):
    held = bands[...].reshape(128, 36).astype(F32).T
    label = lax.broadcasted_iota(jnp.int32, (NBANDS, 128), 0).astype(F32)
    found = jnp.zeros((NBANDS, 128), F32)
    for n in range(36):
        found += (held[n : n + 1] == label).astype(F32)
    scale = 2.0 * jnp.sum(found, axis=1, keepdims=True)
    total = jnp.sum(blocks[...].reshape(32, NY, 8, 128), axis=1).reshape(HALF, 128).T
    for c in range(2):
        for half in range(2):
            at = HALF * c + 128 * half
            power[:, at : at + 128] = (
                total[NBANDS * half : NBANDS * half + NBANDS, 128 * c : 128 * c + 128] / scale
            )
    value = power[...]
    centered = value - jnp.mean(value, axis=1, keepdims=True)
    fisher[...] = lax.dot_general(
        centered,
        centered,
        (((1,), (1,)), ((), ())),
        precision=lax.Precision.HIGHEST,
        preferred_element_type=F32,
    ) * (NMODES / NBANDS / NMAPS)


def per_device(inv_cov, sim_maps, templates, band_index):
    y = lax.axis_index("y")
    zh = lax.axis_index("zh")
    c = lax.axis_index("c")

    gathered = lax.all_gather(sim_maps, BLK, axis=0, tiled=True)

    spans = jnp.stack([templates[:, n * SPAN : (n + 1) * SPAN] for n in range(NY)])
    own = lax.all_to_all(spans, "y", 0, 0, tiled=True)

    a_high, a_low = split_rows(inv_cov)
    gathered, a_high, a_low, own = lax.optimization_barrier((gathered, a_high, a_low, own))

    got = {}
    for dy in (2, 1, 3, 0):
        to = lax.rem(y + dy, NY) * 2
        far, near = rows_of(to + 1 - zh, to + zh, a_high, a_low, gathered)
        if dy == 3:
            far, near, *got[2] = lax.optimization_barrier((far, near, *got[2]))
        got[dy] = [shift(far, dy, 1), shift(near, dy, 0) if dy else near]
        gathered, a_high = lax.optimization_barrier((gathered, a_high, far))[:2]
    sent = [value for dy in (2, 1, 3, 0) for value in got[dy]]
    rows = sent[0]
    for value in sent[1:]:
        rows = rows + value

    keep = lax.dynamic_slice(rows, (0, c * HALF), (ROWS, HALF))
    give = lax.dynamic_slice(rows, (0, (1 - c) * HALF), (ROWS, HALF))
    pair = jnp.stack([keep, swap(give)])
    pair, own, band_index = lax.optimization_barrier((pair, own, band_index))
    other = swap(own)
    around = [shift(pair, dy, 0) if dy else pair for dy in range(NY)]
    bands = lax.all_to_all(
        jnp.broadcast_to(band_index[None, None, :], (128, 1, 36)), EVERY, 0, 0, tiled=True
    )
    held = [lax.rem(y + NY - dy, NY) for dy in range(NY)]
    projected = project(held[:1], around[:1], own, other)
    projected = project(held[1::2], around[1::2], own, other, projected)
    projected = project(held[2:3], around[2:3], own, other, projected)

    projected, bands = lax.optimization_barrier((projected, bands))
    pieces = lax.all_to_all(projected, CHIPS, 0, 0, tiled=True)

    sums = pl.pallas_call(
        band_body,
        in_specs=[
            pl.BlockSpec(memory_space=pltpu.SMEM),
            pl.BlockSpec(memory_space=pltpu.VMEM),
            pl.BlockSpec(memory_space=pltpu.VMEM),
        ],
        out_shape=jax.ShapeDtypeStruct((128, 8, 128), F32),
        compiler_params=limit(32),
    )(jnp.reshape(y, (1,)).astype(jnp.int32), pieces, bands)
    blocks = lax.all_to_all(sums, ("c",) + CHIPS + ("y",), 0, 0, tiled=True)
    return pl.pallas_call(
        final_body,
        out_shape=[
            jax.ShapeDtypeStruct((NBANDS, NMAPS), F32),
            jax.ShapeDtypeStruct((NBANDS, NBANDS), F32),
        ],
        compiler_params=limit(32),
    )(blocks, bands)


def solution(mesh):
    parts = Mesh(mesh.devices.reshape(4, 2, 2, 4, 2), EVERY)
    placed = (P(BLK, RING), P(RING + BLK, None), P(BLK + RING, None), P(BLK + RING))
    body = jax.shard_map(
        per_device, mesh=parts, in_specs=placed, out_specs=(P(), P()), check_vma=False
    )
    return lambda *arrays: tuple(body(*arrays))
```

```python
import jax
import jax.numpy as jnp
from jax import lax
from jax.experimental import pallas as pl
from jax.experimental.pallas import tpu as pltpu
from jax.sharding import Mesh, PartitionSpec as P

NMODES = 4608
NBANDS = 48
NMAPS = 512
NY = 4
SPAN = NMODES // NY
HALF = NMAPS // 2
ROWS = 192
BLK = ("x", "zl", "c")
RING = ("y", "zh")
CHIPS = ("x", "zh", "zl")
EVERY = BLK + RING
MIB = 2**20
F32 = jnp.float32
BF16 = jnp.bfloat16


def split(value):
    high = value.astype(BF16)
    return high, (value - high.astype(F32)).astype(BF16)


def dot(a, b):
    return jnp.dot(a, b, preferred_element_type=F32)


def limit(mib):
    return pltpu.CompilerParams(vmem_limit_bytes=mib * MIB)


def shift(value, dy, dz):
    pairs = [
        (y * 2 + z, ((y + dy) % NY) * 2 + (z + dz) % 2)
        for y in range(NY)
        for z in range(2)
    ]
    return lax.ppermute(value, RING, pairs)


def ring(dy):
    return [(n, (n + dy) % NY) for n in range(NY)]


def swap(value):
    return lax.ppermute(value, "c", [(0, 1), (1, 0)])


def split_body(a, high, low):
    high[...], low[...] = split(a[...])


def split_rows(a):
    rows, cols = a.shape
    step = 128
    block = pl.BlockSpec((step, cols), lambda i: (i, 0))
    return pl.pallas_call(
        split_body,
        grid=(rows // step,),
        in_specs=[block],
        out_specs=[block] * 2,
        out_shape=[jax.ShapeDtypeStruct(a.shape, BF16)] * 2,
        compiler_params=limit(58),
        cost_estimate=pl.CostEstimate(
            flops=2 * rows * cols, bytes_accessed=8 * rows * cols, transcendentals=0
        ),
    )(a)


def add_step(out, value):
    @pl.when(pl.program_id(0) == 0)
    def _():
        out[...] = value

    @pl.when(pl.program_id(0) > 0)
    def _():
        out[...] += value


def row_body(at, far_high, near_high, far_low, near_low, s, far, near):
    sh, sl = split(s[...])
    ah = jnp.concatenate([far_high[...], near_high[...]], axis=0)
    al = jnp.concatenate([far_low[...], near_low[...]], axis=0)
    found = dot(ah, sh) + dot(ah, sl) + dot(al, sh)
    add_step(far, found[:ROWS])
    add_step(near, found[ROWS:])


def rows_of(far, near, a_high, a_low, maps):
    inner, cols = maps.shape
    step = 1024
    a_blocks = [pl.BlockSpec((ROWS, step), lambda k, at, n=n: (at[n], k)) for n in range(2)]
    o_block = pl.BlockSpec((ROWS, cols), lambda k, at: (0, 0))
    return pl.pallas_call(
        row_body,
        grid_spec=pltpu.PrefetchScalarGridSpec(
            num_scalar_prefetch=1,
            grid=(inner // step,),
            in_specs=a_blocks * 2 + [pl.BlockSpec((step, cols), lambda k, at: (k, 0))],
            out_specs=[o_block] * 2,
        ),
        out_shape=[jax.ShapeDtypeStruct((ROWS, cols), F32)] * 2,
        compiler_params=limit(58),
        cost_estimate=pl.CostEstimate(
            flops=12 * ROWS * inner * cols,
            bytes_accessed=4 * inner * (2 * ROWS + cols),
            transcendentals=0,
        ),
    )(jnp.stack([far, near]).astype(jnp.int32), a_high, a_high, a_low, a_low, maps)


def project_body(terms, begun, *refs):
    out = refs[-1]
    cols = 384
    left = []
    for t in range(terms):
        w = refs[3 * t]
        wh, wl = split(jnp.concatenate([w[0], w[1]], axis=0).T)
        left.append(jnp.concatenate([wh, wh, wl], axis=1))
    for n in range(0, SPAN, cols):
        total = None
        for t in range(terms):
            own, other = refs[3 * t + 1 : 3 * t + 3]
            th, tl = split(
                jnp.concatenate([own[0, :, n : n + cols], other[0, :, n : n + cols]], axis=0)
            )
            term = dot(left[t], jnp.concatenate([th, tl, th], axis=0))
            total = term if total is None else total + term
        for half in range(2):
            part = total[128 * half : 128 * half + 128].reshape(16, 8, cols)
            if begun:
                part += refs[3 * terms][:, half, :, n : n + cols]
            out[:, half, :, n : n + cols] = part


def project(at, weighted, own, other, begun=None):
    terms = len(weighted)
    operands = [v for w in weighted for v in (w, own, other)]
    in_specs = []
    for t in range(terms):
        block = pl.BlockSpec((1, ROWS, SPAN), lambda i, t=t: (at[t], 0, 0))
        in_specs += [pl.BlockSpec((2, ROWS, HALF), lambda i: (0, 0, 0)), block, block]
    whole = pl.BlockSpec((16, 2, 8, SPAN), lambda i: (0, 0, 0, 0))
    if begun is not None:
        operands.append(begun)
        in_specs.append(whole)

    def body(*refs):
        project_body(terms, begun is not None, *refs)

    return pl.pallas_call(
        body,
        grid=(1,),
        in_specs=in_specs,
        out_specs=whole,
        out_shape=jax.ShapeDtypeStruct((16, 2, 8, SPAN), F32),
        compiler_params=limit(32),
        cost_estimate=pl.CostEstimate(
            flops=terms * 6 * 2 * ROWS * HALF * SPAN,
            bytes_accessed=8 * terms * ROWS * SPAN,
            transcendentals=0,
        ),
    )(*operands)


def names_row():
    lane = lax.broadcasted_iota(jnp.int32, (1, 128), 1)
    return jnp.where(
        lane < NBANDS, lane, jnp.where(lane < 2 * NBANDS, lane - NBANDS, -1)
    ).astype(F32)


def band_body(y, pieces, bands, out):
    devices, each = SPAN // 36, 36
    held = bands[pl.ds(y[0] * devices, devices)].reshape(devices, each).astype(F32)
    row = lax.broadcasted_iota(jnp.int32, (SPAN, devices), 0)
    begin = lax.broadcasted_iota(jnp.int32, (SPAN, devices), 1) * each
    source = ((row >= begin) & (row < begin + each)).astype(F32)
    start = jnp.sum(source * begin.astype(F32), axis=1, keepdims=True)
    at = lax.broadcasted_iota(jnp.int32, (SPAN, each), 0).astype(F32) - start
    mask = at == lax.broadcasted_iota(jnp.int32, (SPAN, each), 1).astype(F32)
    spread = jnp.dot(source, held, preferred_element_type=F32)
    band = jnp.sum(jnp.where(mask, spread, 0.0), axis=1, keepdims=True)
    onehot = (band == names_row()).astype(F32)

    modes = jnp.sum(pieces[...], axis=0)
    sums = jnp.dot(
        (modes * modes).reshape(16, SPAN),
        onehot,
        precision=lax.Precision.HIGHEST,
        preferred_element_type=F32,
    )
    lane = lax.broadcasted_iota(jnp.int32, (8, 128), 1)
    both = jnp.where(lane < NBANDS, sums[:8], sums[8:])
    out[...] = jnp.broadcast_to(both[None], out.shape)


def final_body(blocks, bands, power, fisher):
    held = bands[...].reshape(128, 36).astype(F32).T
    label = lax.broadcasted_iota(jnp.int32, (NBANDS, 128), 0).astype(F32)
    found = jnp.zeros((NBANDS, 128), F32)
    for n in range(36):
        found += (held[n : n + 1] == label).astype(F32)
    scale = 2.0 * jnp.sum(found, axis=1, keepdims=True)
    total = jnp.sum(blocks[...].reshape(32, NY, 8, 128), axis=1).reshape(HALF, 128).T
    for c in range(2):
        for half in range(2):
            at = HALF * c + 128 * half
            power[:, at : at + 128] = (
                total[NBANDS * half : NBANDS * half + NBANDS, 128 * c : 128 * c + 128] / scale
            )
    value = power[...]
    centered = value - jnp.mean(value, axis=1, keepdims=True)
    fisher[...] = lax.dot_general(
        centered,
        centered,
        (((1,), (1,)), ((), ())),
        precision=lax.Precision.HIGHEST,
        preferred_element_type=F32,
    ) * (NMODES / NBANDS / NMAPS)


def per_device(inv_cov, sim_maps, templates, band_index):
    y = lax.axis_index("y")
    zh = lax.axis_index("zh")
    c = lax.axis_index("c")

    gathered = lax.all_gather(sim_maps, BLK, axis=0, tiled=True)

    columns = []
    for dy in range(NY):
        block = lax.dynamic_slice(templates, (0, lax.rem(y + dy, NY) * SPAN), (ROWS, SPAN))
        columns.append(lax.ppermute(block, "y", ring(dy)) if dy else block)

    bands = lax.all_to_all(
        jnp.broadcast_to(band_index[None, None, :], (128, 1, 36)), EVERY, 0, 0, tiled=True
    )
    a_high, a_low = split_rows(inv_cov)
    gathered, a_high, a_low, bands, *columns = lax.optimization_barrier(
        (gathered, a_high, a_low, bands, *columns)
    )

    got = {}
    for dy in (2, 1, 3, 0):
        to = lax.rem(y + dy, NY) * 2
        far, near = rows_of(to + 1 - zh, to + zh, a_high, a_low, gathered)
        if dy == 3:
            far, near, *got[2] = lax.optimization_barrier((far, near, *got[2]))
        got[dy] = [shift(far, dy, 1), shift(near, dy, 0) if dy else near]
        gathered, a_high = lax.optimization_barrier((gathered, a_high, far))[:2]
    sent = [value for dy in (2, 1, 3, 0) for value in got[dy]]
    sent[-1], *columns = lax.optimization_barrier((sent[-1], *columns))
    own = jnp.stack(columns)
    *sent, own = lax.optimization_barrier((*sent, own))
    rows = sent[0]
    for value in sent[1:]:
        rows = rows + value

    keep = lax.dynamic_slice(rows, (0, c * HALF), (ROWS, HALF))
    give = lax.dynamic_slice(rows, (0, (1 - c) * HALF), (ROWS, HALF))
    pair = jnp.stack([keep, swap(give)])
    pair, own = lax.optimization_barrier((pair, own))
    other = swap(own)
    around = [shift(pair, dy, 0) if dy else pair for dy in range(NY)]
    projected = project((0,), around[:1], own, other)
    projected = project((1, 3), around[1::2], own, other, projected)
    projected = project((2,), around[2:3], own, other, projected)

    pieces = lax.all_to_all(projected, CHIPS, 0, 0, tiled=True)

    sums = pl.pallas_call(
        band_body,
        in_specs=[
            pl.BlockSpec(memory_space=pltpu.SMEM),
            pl.BlockSpec(memory_space=pltpu.VMEM),
            pl.BlockSpec(memory_space=pltpu.VMEM),
        ],
        out_shape=jax.ShapeDtypeStruct((128, 8, 128), F32),
        compiler_params=limit(32),
    )(jnp.reshape(y, (1,)).astype(jnp.int32), pieces, bands)
    blocks = lax.all_to_all(sums, ("c",) + CHIPS + ("y",), 0, 0, tiled=True)
    return pl.pallas_call(
        final_body,
        out_shape=[
            jax.ShapeDtypeStruct((NBANDS, NMAPS), F32),
            jax.ShapeDtypeStruct((NBANDS, NBANDS), F32),
        ],
        compiler_params=limit(32),
    )(blocks, bands)


def solution(mesh):
    parts = Mesh(mesh.devices.reshape(4, 2, 2, 4, 2), EVERY)
    placed = (P(BLK, RING), P(RING + BLK, None), P(BLK + RING, None), P(BLK + RING))
    body = jax.shard_map(
        per_device, mesh=parts, in_specs=placed, out_specs=(P(), P()), check_vma=False
    )
    return lambda *arrays: tuple(body(*arrays))
```

```python
import jax
import jax.numpy as jnp
from jax import lax
from jax.experimental import pallas as pl
from jax.experimental.pallas import tpu as pltpu
from jax.sharding import Mesh, PartitionSpec as P

NMODES = 4608
NBANDS = 48
NMAPS = 512
NY = 4
SPAN = NMODES // NY
HALF = NMAPS // 2
ROWS = 192
BLK = ("x", "zl", "c")
RING = ("y", "zh")
CHIPS = ("x", "zh", "zl")
EVERY = BLK + RING
MIB = 2**20
F32 = jnp.float32
BF16 = jnp.bfloat16


def split(value):
    high = value.astype(BF16)
    return high, (value - high.astype(F32)).astype(BF16)


def dot(a, b):
    return jnp.dot(a, b, preferred_element_type=F32)


def limit(mib):
    return pltpu.CompilerParams(vmem_limit_bytes=mib * MIB)


def shift(value, dy, dz):
    pairs = [
        (y * 2 + z, ((y + dy) % NY) * 2 + (z + dz) % 2)
        for y in range(NY)
        for z in range(2)
    ]
    return lax.ppermute(value, RING, pairs)


def ring(dy):
    return [(n, (n + dy) % NY) for n in range(NY)]


def swap(value):
    return lax.ppermute(value, "c", [(0, 1), (1, 0)])


def split_body(a, high, low):
    high[...], low[...] = split(a[...])


def split_rows(a):
    rows, cols = a.shape
    step = 128
    block = pl.BlockSpec((step, cols), lambda i: (i, 0))
    return pl.pallas_call(
        split_body,
        grid=(rows // step,),
        in_specs=[block],
        out_specs=[block] * 2,
        out_shape=[jax.ShapeDtypeStruct(a.shape, BF16)] * 2,
        compiler_params=limit(20),
        cost_estimate=pl.CostEstimate(
            flops=2 * rows * cols, bytes_accessed=8 * rows * cols, transcendentals=0
        ),
    )(a)


def add_step(out, value):
    @pl.when(pl.program_id(0) == 0)
    def _():
        out[...] = value

    @pl.when(pl.program_id(0) > 0)
    def _():
        out[...] += value


def row_body(at, a_high, a_low, s, far, near):
    sh, sl = split(s[...])
    ah = a_high[...]
    found = dot(ah, sh) + dot(ah, sl) + dot(a_low[...], sh)
    first, second = found[:ROWS], found[ROWS:]
    swapped = at[1] == 0
    add_step(far, jnp.where(swapped, second, first))
    add_step(near, jnp.where(swapped, first, second))


def rows_of(to, zh, a_high, a_low, maps):
    inner, cols = maps.shape
    step = 1024
    a_block = pl.BlockSpec((2 * ROWS, step), lambda k, at: (at[0], k))
    o_block = pl.BlockSpec((ROWS, cols), lambda k, at: (0, 0))
    return pl.pallas_call(
        row_body,
        grid_spec=pltpu.PrefetchScalarGridSpec(
            num_scalar_prefetch=1,
            grid=(inner // step,),
            in_specs=[a_block, a_block, pl.BlockSpec((step, cols), lambda k, at: (k, 0))],
            out_specs=[o_block] * 2,
        ),
        out_shape=[jax.ShapeDtypeStruct((ROWS, cols), F32)] * 2,
        compiler_params=limit(20),
        cost_estimate=pl.CostEstimate(
            flops=12 * ROWS * inner * cols,
            bytes_accessed=4 * inner * (2 * ROWS + cols),
            transcendentals=0,
        ),
    )(jnp.stack([to, zh]).astype(jnp.int32), a_high, a_low, maps)


def project_body(terms, begun, *refs):
    out = refs[-1]
    cols = 384
    left = []
    for t in range(terms):
        w = refs[3 * t]
        wh, wl = split(jnp.concatenate([w[0], w[1]], axis=0).T)
        left.append(jnp.concatenate([wh, wh, wl], axis=1))
    for n in range(0, SPAN, cols):
        total = None
        for t in range(terms):
            own, other = refs[3 * t + 1 : 3 * t + 3]
            th, tl = split(
                jnp.concatenate([own[0, :, n : n + cols], other[0, :, n : n + cols]], axis=0)
            )
            term = dot(left[t], jnp.concatenate([th, tl, th], axis=0))
            total = term if total is None else total + term
        for half in range(2):
            part = total[128 * half : 128 * half + 128].reshape(16, 8, cols)
            if begun:
                part += refs[3 * terms][:, half, :, n : n + cols]
            out[:, half, :, n : n + cols] = part


def project(at, weighted, own, other, begun=None):
    terms = len(weighted)
    operands = [v for w in weighted for v in (w, own, other)]
    in_specs = []
    for t in range(terms):
        block = pl.BlockSpec((1, ROWS, SPAN), lambda i, t=t: (at[t], 0, 0))
        in_specs += [pl.BlockSpec((2, ROWS, HALF), lambda i: (0, 0, 0)), block, block]
    whole = pl.BlockSpec((16, 2, 8, SPAN), lambda i: (0, 0, 0, 0))
    if begun is not None:
        operands.append(begun)
        in_specs.append(whole)

    def body(*refs):
        project_body(terms, begun is not None, *refs)

    return pl.pallas_call(
        body,
        grid=(1,),
        in_specs=in_specs,
        out_specs=whole,
        out_shape=jax.ShapeDtypeStruct((16, 2, 8, SPAN), F32),
        compiler_params=limit(32),
        cost_estimate=pl.CostEstimate(
            flops=terms * 6 * 2 * ROWS * HALF * SPAN,
            bytes_accessed=8 * terms * ROWS * SPAN,
            transcendentals=0,
        ),
    )(*operands)


def names_row():
    lane = lax.broadcasted_iota(jnp.int32, (1, 128), 1)
    return jnp.where(
        lane < NBANDS, lane, jnp.where(lane < 2 * NBANDS, lane - NBANDS, -1)
    ).astype(F32)


def band_body(y, pieces, bands, out):
    devices, each = SPAN // 36, 36
    held = bands[pl.ds(y[0] * devices, devices)].reshape(devices, each).astype(F32)
    row = lax.broadcasted_iota(jnp.int32, (SPAN, devices), 0)
    begin = lax.broadcasted_iota(jnp.int32, (SPAN, devices), 1) * each
    source = ((row >= begin) & (row < begin + each)).astype(F32)
    start = jnp.sum(source * begin.astype(F32), axis=1, keepdims=True)
    at = lax.broadcasted_iota(jnp.int32, (SPAN, each), 0).astype(F32) - start
    mask = at == lax.broadcasted_iota(jnp.int32, (SPAN, each), 1).astype(F32)
    spread = jnp.dot(source, held, preferred_element_type=F32)
    band = jnp.sum(jnp.where(mask, spread, 0.0), axis=1, keepdims=True)
    onehot = (band == names_row()).astype(F32)

    modes = jnp.sum(pieces[...], axis=0)
    sums = jnp.dot(
        (modes * modes).reshape(16, SPAN),
        onehot,
        precision=lax.Precision.HIGHEST,
        preferred_element_type=F32,
    )
    lane = lax.broadcasted_iota(jnp.int32, (8, 128), 1)
    both = jnp.where(lane < NBANDS, sums[:8], sums[8:])
    out[...] = jnp.broadcast_to(both[None], out.shape)


def final_body(blocks, bands, power, fisher):
    held = bands[...].reshape(128, 36).astype(F32).T
    label = lax.broadcasted_iota(jnp.int32, (NBANDS, 128), 0).astype(F32)
    found = jnp.zeros((NBANDS, 128), F32)
    for n in range(36):
        found += (held[n : n + 1] == label).astype(F32)
    scale = 2.0 * jnp.sum(found, axis=1, keepdims=True)
    total = jnp.sum(blocks[...].reshape(32, NY, 8, 128), axis=1).reshape(HALF, 128).T
    for c in range(2):
        for half in range(2):
            at = HALF * c + 128 * half
            power[:, at : at + 128] = (
                total[NBANDS * half : NBANDS * half + NBANDS, 128 * c : 128 * c + 128] / scale
            )
    value = power[...]
    centered = value - jnp.mean(value, axis=1, keepdims=True)
    fisher[...] = lax.dot_general(
        centered,
        centered,
        (((1,), (1,)), ((), ())),
        precision=lax.Precision.HIGHEST,
        preferred_element_type=F32,
    ) * (NMODES / NBANDS / NMAPS)


def per_device(inv_cov, sim_maps, templates, band_index):
    y = lax.axis_index("y")
    zh = lax.axis_index("zh")
    c = lax.axis_index("c")

    gathered = lax.all_gather(sim_maps, BLK, axis=0, tiled=True)

    columns = []
    for dy in range(NY):
        block = lax.dynamic_slice(templates, (0, lax.rem(y + dy, NY) * SPAN), (ROWS, SPAN))
        columns.append(lax.ppermute(block, "y", ring(dy)) if dy else block)

    bands = lax.all_to_all(
        jnp.broadcast_to(band_index[None, None, :], (128, 1, 36)), EVERY, 0, 0, tiled=True
    )
    a_high, a_low = split_rows(inv_cov)
    gathered, bands, *columns = lax.optimization_barrier((gathered, bands, *columns))

    got = {}
    for dy in (2, 1, 3, 0):
        far, near = rows_of(lax.rem(y + dy, NY), zh, a_high, a_low, gathered)
        if dy == 3:
            far, near, *got[2] = lax.optimization_barrier((far, near, *got[2]))
        got[dy] = [shift(far, dy, 1), shift(near, dy, 0) if dy else near]
        gathered, far = lax.optimization_barrier((gathered, far))
    sent = [value for dy in (2, 1, 3, 0) for value in got[dy]]
    sent[-1], *columns = lax.optimization_barrier((sent[-1], *columns))
    own = jnp.stack(columns)
    *sent, own = lax.optimization_barrier((*sent, own))
    rows = sent[0]
    for value in sent[1:]:
        rows = rows + value

    keep = lax.dynamic_slice(rows, (0, c * HALF), (ROWS, HALF))
    give = lax.dynamic_slice(rows, (0, (1 - c) * HALF), (ROWS, HALF))
    pair = jnp.stack([keep, swap(give)])
    pair, own = lax.optimization_barrier((pair, own))
    other = swap(own)
    around = [shift(pair, dy, 0) if dy else pair for dy in range(NY)]
    projected = project((0,), around[:1], own, other)
    projected = project((1, 3), around[1::2], own, other, projected)
    projected = project((2,), around[2:3], own, other, projected)

    pieces = lax.all_to_all(projected, CHIPS, 0, 0, tiled=True)

    sums = pl.pallas_call(
        band_body,
        in_specs=[
            pl.BlockSpec(memory_space=pltpu.SMEM),
            pl.BlockSpec(memory_space=pltpu.VMEM),
            pl.BlockSpec(memory_space=pltpu.VMEM),
        ],
        out_shape=jax.ShapeDtypeStruct((128, 8, 128), F32),
        compiler_params=limit(32),
    )(jnp.reshape(y, (1,)).astype(jnp.int32), pieces, bands)
    blocks = lax.all_to_all(sums, ("c",) + CHIPS + ("y",), 0, 0, tiled=True)
    return pl.pallas_call(
        final_body,
        out_shape=[
            jax.ShapeDtypeStruct((NBANDS, NMAPS), F32),
            jax.ShapeDtypeStruct((NBANDS, NBANDS), F32),
        ],
        compiler_params=limit(32),
    )(blocks, bands)


def solution(mesh):
    parts = Mesh(mesh.devices.reshape(4, 2, 2, 4, 2), EVERY)
    placed = (P(BLK, RING), P(RING + BLK, None), P(BLK + RING, None), P(BLK + RING))
    body = jax.shard_map(
        per_device, mesh=parts, in_specs=placed, out_specs=(P(), P()), check_vma=False
    )
    return lambda *arrays: tuple(body(*arrays))
```

```python
import jax
import jax.numpy as jnp
from jax import lax
from jax.experimental import pallas as pl
from jax.experimental.pallas import tpu as pltpu
from jax.sharding import Mesh, PartitionSpec as P

NMODES = 4608
NBANDS = 48
NMAPS = 512
NY = 4
SPAN = NMODES // NY
HALF = NMAPS // 2
ROWS = 192
BLK = ("x", "zl", "c")
RING = ("y", "zh")
CHIPS = ("x", "zh", "zl")
EVERY = BLK + RING
MIB = 2**20
F32 = jnp.float32
BF16 = jnp.bfloat16


def split(value):
    high = value.astype(BF16)
    return high, (value - high.astype(F32)).astype(BF16)


def dot(a, b):
    return jnp.dot(a, b, preferred_element_type=F32)


def limit(mib):
    return pltpu.CompilerParams(vmem_limit_bytes=mib * MIB)


def shift(value, dy, dz):
    pairs = [
        (y * 2 + z, ((y + dy) % NY) * 2 + (z + dz) % 2)
        for y in range(NY)
        for z in range(2)
    ]
    return lax.ppermute(value, RING, pairs)


def ring(dy):
    return [(n, (n + dy) % NY) for n in range(NY)]


def swap(value):
    return lax.ppermute(value, "c", [(0, 1), (1, 0)])


def split_body(a, high, low):
    high[...], low[...] = split(a[...])


def split_rows(a):
    rows, cols = a.shape
    step = 128
    block = pl.BlockSpec((step, cols), lambda i: (i, 0))
    return pl.pallas_call(
        split_body,
        grid=(rows // step,),
        in_specs=[block],
        out_specs=[block] * 2,
        out_shape=[jax.ShapeDtypeStruct(a.shape, BF16)] * 2,
        compiler_params=limit(58),
        cost_estimate=pl.CostEstimate(
            flops=2 * rows * cols, bytes_accessed=8 * rows * cols, transcendentals=0
        ),
    )(a)


def add_step(out, value):
    @pl.when(pl.program_id(0) == 0)
    def _():
        out[...] = value

    @pl.when(pl.program_id(0) > 0)
    def _():
        out[...] += value


def row_body(at, a_high, a_low, s, far, near):
    sh, sl = split(s[...])
    ah = a_high[...]
    found = dot(ah, sh) + dot(ah, sl) + dot(a_low[...], sh)
    first, second = found[:ROWS], found[ROWS:]
    swapped = at[1] == 0
    add_step(far, jnp.where(swapped, second, first))
    add_step(near, jnp.where(swapped, first, second))


def rows_of(to, zh, a_high, a_low, maps):
    inner, cols = maps.shape
    step = 1536
    a_block = pl.BlockSpec((2 * ROWS, step), lambda k, at: (at[0], k))
    o_block = pl.BlockSpec((ROWS, cols), lambda k, at: (0, 0))
    return pl.pallas_call(
        row_body,
        grid_spec=pltpu.PrefetchScalarGridSpec(
            num_scalar_prefetch=1,
            grid=(inner // step,),
            in_specs=[a_block, a_block, pl.BlockSpec((step, cols), lambda k, at: (k, 0))],
            out_specs=[o_block] * 2,
        ),
        out_shape=[jax.ShapeDtypeStruct((ROWS, cols), F32)] * 2,
        compiler_params=limit(58),
        cost_estimate=pl.CostEstimate(
            flops=12 * ROWS * inner * cols,
            bytes_accessed=4 * inner * (2 * ROWS + cols),
            transcendentals=0,
        ),
    )(jnp.stack([to, zh]).astype(jnp.int32), a_high, a_low, maps)


def project_body(terms, begun, *refs):
    out = refs[-1]
    cols = 384
    left = []
    for t in range(terms):
        w = refs[3 * t]
        wh, wl = split(jnp.concatenate([w[0], w[1]], axis=0).T)
        left.append(jnp.concatenate([wh, wh, wl], axis=1))
    for n in range(0, SPAN, cols):
        total = None
        for t in range(terms):
            own, other = refs[3 * t + 1 : 3 * t + 3]
            th, tl = split(
                jnp.concatenate([own[0, :, n : n + cols], other[0, :, n : n + cols]], axis=0)
            )
            term = dot(left[t], jnp.concatenate([th, tl, th], axis=0))
            total = term if total is None else total + term
        for half in range(2):
            part = total[128 * half : 128 * half + 128].reshape(16, 8, cols)
            if begun:
                part += refs[3 * terms][:, half, :, n : n + cols]
            out[:, half, :, n : n + cols] = part


def project(at, weighted, own, other, begun=None):
    terms = len(weighted)
    operands = [v for w in weighted for v in (w, own, other)]
    in_specs = []
    for t in range(terms):
        block = pl.BlockSpec((1, ROWS, SPAN), lambda i, t=t: (at[t], 0, 0))
        in_specs += [pl.BlockSpec((2, ROWS, HALF), lambda i: (0, 0, 0)), block, block]
    whole = pl.BlockSpec((16, 2, 8, SPAN), lambda i: (0, 0, 0, 0))
    if begun is not None:
        operands.append(begun)
        in_specs.append(whole)

    def body(*refs):
        project_body(terms, begun is not None, *refs)

    return pl.pallas_call(
        body,
        grid=(1,),
        in_specs=in_specs,
        out_specs=whole,
        out_shape=jax.ShapeDtypeStruct((16, 2, 8, SPAN), F32),
        compiler_params=limit(32),
        cost_estimate=pl.CostEstimate(
            flops=terms * 6 * 2 * ROWS * HALF * SPAN,
            bytes_accessed=8 * terms * ROWS * SPAN,
            transcendentals=0,
        ),
    )(*operands)


def names_row():
    lane = lax.broadcasted_iota(jnp.int32, (1, 128), 1)
    return jnp.where(
        lane < NBANDS, lane, jnp.where(lane < 2 * NBANDS, lane - NBANDS, -1)
    ).astype(F32)


def band_body(y, pieces, bands, out):
    devices, each = SPAN // 36, 36
    held = bands[pl.ds(y[0] * devices, devices)].reshape(devices, each).astype(F32)
    row = lax.broadcasted_iota(jnp.int32, (SPAN, devices), 0)
    begin = lax.broadcasted_iota(jnp.int32, (SPAN, devices), 1) * each
    source = ((row >= begin) & (row < begin + each)).astype(F32)
    start = jnp.sum(source * begin.astype(F32), axis=1, keepdims=True)
    at = lax.broadcasted_iota(jnp.int32, (SPAN, each), 0).astype(F32) - start
    mask = at == lax.broadcasted_iota(jnp.int32, (SPAN, each), 1).astype(F32)
    spread = jnp.dot(source, held, preferred_element_type=F32)
    band = jnp.sum(jnp.where(mask, spread, 0.0), axis=1, keepdims=True)
    onehot = (band == names_row()).astype(F32)

    modes = jnp.sum(pieces[...], axis=0)
    sums = jnp.dot(
        (modes * modes).reshape(16, SPAN),
        onehot,
        precision=lax.Precision.HIGHEST,
        preferred_element_type=F32,
    )
    lane = lax.broadcasted_iota(jnp.int32, (8, 128), 1)
    both = jnp.where(lane < NBANDS, sums[:8], sums[8:])
    out[...] = jnp.broadcast_to(both[None], out.shape)


def final_body(blocks, bands, power, fisher):
    held = bands[...].reshape(128, 36).astype(F32).T
    label = lax.broadcasted_iota(jnp.int32, (NBANDS, 128), 0).astype(F32)
    found = jnp.zeros((NBANDS, 128), F32)
    for n in range(36):
        found += (held[n : n + 1] == label).astype(F32)
    scale = 2.0 * jnp.sum(found, axis=1, keepdims=True)
    total = jnp.sum(blocks[...].reshape(32, NY, 8, 128), axis=1).reshape(HALF, 128).T
    for c in range(2):
        for half in range(2):
            at = HALF * c + 128 * half
            power[:, at : at + 128] = (
                total[NBANDS * half : NBANDS * half + NBANDS, 128 * c : 128 * c + 128] / scale
            )
    value = power[...]
    centered = value - jnp.mean(value, axis=1, keepdims=True)
    fisher[...] = lax.dot_general(
        centered,
        centered,
        (((1,), (1,)), ((), ())),
        precision=lax.Precision.HIGHEST,
        preferred_element_type=F32,
    ) * (NMODES / NBANDS / NMAPS)


def per_device(inv_cov, sim_maps, templates, band_index):
    y = lax.axis_index("y")
    zh = lax.axis_index("zh")
    c = lax.axis_index("c")

    gathered = lax.all_gather(sim_maps, BLK, axis=0, tiled=True)

    columns = []
    for dy in range(NY):
        block = lax.dynamic_slice(templates, (0, lax.rem(y + dy, NY) * SPAN), (ROWS, SPAN))
        columns.append(lax.ppermute(block, "y", ring(dy)) if dy else block)

    bands = lax.all_to_all(
        jnp.broadcast_to(band_index[None, None, :], (128, 1, 36)), EVERY, 0, 0, tiled=True
    )
    a_high, a_low = split_rows(inv_cov)
    gathered, a_high, a_low = lax.optimization_barrier((gathered, a_high, a_low))

    got = {}
    for dy in (2, 1, 3, 0):
        far, near = rows_of(lax.rem(y + dy, NY), zh, a_high, a_low, gathered)
        if dy == 2:
            far, near, bands, *columns = lax.optimization_barrier((far, near, bands, *columns))
        if dy == 3:
            far, near, *got[2] = lax.optimization_barrier((far, near, *got[2]))
        got[dy] = [shift(far, dy, 1), shift(near, dy, 0) if dy else near]
        gathered, a_high = lax.optimization_barrier((gathered, a_high, far))[:2]
    sent = [value for dy in (2, 1, 3, 0) for value in got[dy]]
    sent[-1], *columns = lax.optimization_barrier((sent[-1], *columns))
    own = jnp.stack(columns)
    *sent, own = lax.optimization_barrier((*sent, own))
    rows = sent[0]
    for value in sent[1:]:
        rows = rows + value

    keep = lax.dynamic_slice(rows, (0, c * HALF), (ROWS, HALF))
    give = lax.dynamic_slice(rows, (0, (1 - c) * HALF), (ROWS, HALF))
    pair = jnp.stack([keep, swap(give)])
    pair, own = lax.optimization_barrier((pair, own))
    other = swap(own)
    around = [shift(pair, dy, 0) if dy else pair for dy in range(NY)]
    projected = project((0,), around[:1], own, other)
    projected = project((1, 3), around[1::2], own, other, projected)
    projected = project((2,), around[2:3], own, other, projected)

    pieces = lax.all_to_all(projected, CHIPS, 0, 0, tiled=True)

    sums = pl.pallas_call(
        band_body,
        in_specs=[
            pl.BlockSpec(memory_space=pltpu.SMEM),
            pl.BlockSpec(memory_space=pltpu.VMEM),
            pl.BlockSpec(memory_space=pltpu.VMEM),
        ],
        out_shape=jax.ShapeDtypeStruct((128, 8, 128), F32),
        compiler_params=limit(32),
    )(jnp.reshape(y, (1,)).astype(jnp.int32), pieces, bands)
    blocks = lax.all_to_all(sums, ("c",) + CHIPS + ("y",), 0, 0, tiled=True)
    return pl.pallas_call(
        final_body,
        out_shape=[
            jax.ShapeDtypeStruct((NBANDS, NMAPS), F32),
            jax.ShapeDtypeStruct((NBANDS, NBANDS), F32),
        ],
        compiler_params=limit(32),
    )(blocks, bands)


def solution(mesh):
    parts = Mesh(mesh.devices.reshape(4, 2, 2, 4, 2), EVERY)
    placed = (P(BLK, RING), P(RING + BLK, None), P(BLK + RING, None), P(BLK + RING))
    body = jax.shard_map(
        per_device, mesh=parts, in_specs=placed, out_specs=(P(), P()), check_vma=False
    )
    return lambda *arrays: tuple(body(*arrays))
```

```python
import jax
import jax.numpy as jnp
from jax import lax
from jax.experimental import pallas as pl
from jax.experimental.pallas import tpu as pltpu
from jax.sharding import Mesh, PartitionSpec as P

NMODES = 4608
NBANDS = 48
NMAPS = 512
NY = 4
SPAN = NMODES // NY
HALF = NMAPS // 2
ROWS = 192
BLK = ("x", "zl", "c")
RING = ("y", "zh")
CHIPS = ("x", "zh", "zl")
EVERY = BLK + RING
MIB = 2**20
F32 = jnp.float32
BF16 = jnp.bfloat16


def split(value):
    high = value.astype(BF16)
    return high, (value - high.astype(F32)).astype(BF16)


def dot(a, b):
    return jnp.dot(a, b, preferred_element_type=F32)


def limit(mib):
    return pltpu.CompilerParams(vmem_limit_bytes=mib * MIB)


def shift(value, dy, dz):
    pairs = [
        (y * 2 + z, ((y + dy) % NY) * 2 + (z + dz) % 2)
        for y in range(NY)
        for z in range(2)
    ]
    return lax.ppermute(value, RING, pairs)


def ring(dy):
    return [(n, (n + dy) % NY) for n in range(NY)]


def swap(value):
    return lax.ppermute(value, "c", [(0, 1), (1, 0)])


def split_body(a, high, low):
    high[...], low[...] = split(a[...])


def split_rows(a):
    rows, cols = a.shape
    step = 128
    block = pl.BlockSpec((step, cols), lambda i: (i, 0))
    return pl.pallas_call(
        split_body,
        grid=(rows // step,),
        in_specs=[block],
        out_specs=[block] * 2,
        out_shape=[jax.ShapeDtypeStruct(a.shape, BF16)] * 2,
        compiler_params=limit(58),
        cost_estimate=pl.CostEstimate(
            flops=2 * rows * cols, bytes_accessed=8 * rows * cols, transcendentals=0
        ),
    )(a)


def add_step(out, value):
    @pl.when(pl.program_id(0) == 0)
    def _():
        out[...] = value

    @pl.when(pl.program_id(0) > 0)
    def _():
        out[...] += value


def row_body(at, a_high, a_low, s, far, near):
    sh, sl = split(s[...])
    ah = a_high[...]
    found = dot(ah, sh) + dot(ah, sl) + dot(a_low[...], sh)
    first, second = found[:ROWS], found[ROWS:]
    swapped = at[1] == 0
    add_step(far, jnp.where(swapped, second, first))
    add_step(near, jnp.where(swapped, first, second))


def rows_of(to, zh, a_high, a_low, maps):
    inner, cols = maps.shape
    step = 1536
    a_block = pl.BlockSpec((2 * ROWS, step), lambda k, at: (at[0], k))
    o_block = pl.BlockSpec((ROWS, cols), lambda k, at: (0, 0))
    return pl.pallas_call(
        row_body,
        grid_spec=pltpu.PrefetchScalarGridSpec(
            num_scalar_prefetch=1,
            grid=(inner // step,),
            in_specs=[a_block, a_block, pl.BlockSpec((step, cols), lambda k, at: (k, 0))],
            out_specs=[o_block] * 2,
        ),
        out_shape=[jax.ShapeDtypeStruct((ROWS, cols), F32)] * 2,
        compiler_params=limit(58),
        cost_estimate=pl.CostEstimate(
            flops=12 * ROWS * inner * cols,
            bytes_accessed=4 * inner * (2 * ROWS + cols),
            transcendentals=0,
        ),
    )(jnp.stack([to, zh]).astype(jnp.int32), a_high, a_low, maps)


def block_body(at, a_high, a_low, s, out):
    sh, sl = split(s[...])
    ah = a_high[...]
    add_step(out, dot(ah, sh) + dot(ah, sl) + dot(a_low[...], sh))


def block_of(at, a_high, a_low, maps):
    inner, cols = maps.shape
    step = 1536
    a_block = pl.BlockSpec((ROWS, step), lambda k, at: (at[0], k))
    return pl.pallas_call(
        block_body,
        grid_spec=pltpu.PrefetchScalarGridSpec(
            num_scalar_prefetch=1,
            grid=(inner // step,),
            in_specs=[a_block, a_block, pl.BlockSpec((step, cols), lambda k, at: (k, 0))],
            out_specs=pl.BlockSpec((ROWS, cols), lambda k, at: (0, 0)),
        ),
        out_shape=jax.ShapeDtypeStruct((ROWS, cols), F32),
        compiler_params=limit(58),
        cost_estimate=pl.CostEstimate(
            flops=6 * ROWS * inner * cols,
            bytes_accessed=4 * inner * (ROWS + cols),
            transcendentals=0,
        ),
    )(jnp.reshape(at, (1,)).astype(jnp.int32), a_high, a_low, maps)


def project_body(terms, begun, *refs):
    out = refs[-1]
    cols = 384
    left = []
    for t in range(terms):
        w = refs[3 * t]
        wh, wl = split(jnp.concatenate([w[0], w[1]], axis=0).T)
        left.append(jnp.concatenate([wh, wh, wl], axis=1))
    for n in range(0, SPAN, cols):
        total = None
        for t in range(terms):
            own, other = refs[3 * t + 1 : 3 * t + 3]
            th, tl = split(
                jnp.concatenate([own[0, :, n : n + cols], other[0, :, n : n + cols]], axis=0)
            )
            term = dot(left[t], jnp.concatenate([th, tl, th], axis=0))
            total = term if total is None else total + term
        for half in range(2):
            part = total[128 * half : 128 * half + 128].reshape(16, 8, cols)
            if begun:
                part += refs[3 * terms][:, half, :, n : n + cols]
            out[:, half, :, n : n + cols] = part


def project(at, weighted, own, other, begun=None):
    terms = len(weighted)
    operands = [v for w in weighted for v in (w, own, other)]
    in_specs = []
    for t in range(terms):
        block = pl.BlockSpec((1, ROWS, SPAN), lambda i, t=t: (at[t], 0, 0))
        in_specs += [pl.BlockSpec((2, ROWS, HALF), lambda i: (0, 0, 0)), block, block]
    whole = pl.BlockSpec((16, 2, 8, SPAN), lambda i: (0, 0, 0, 0))
    if begun is not None:
        operands.append(begun)
        in_specs.append(whole)

    def body(*refs):
        project_body(terms, begun is not None, *refs)

    return pl.pallas_call(
        body,
        grid=(1,),
        in_specs=in_specs,
        out_specs=whole,
        out_shape=jax.ShapeDtypeStruct((16, 2, 8, SPAN), F32),
        compiler_params=limit(32),
        cost_estimate=pl.CostEstimate(
            flops=terms * 6 * 2 * ROWS * HALF * SPAN,
            bytes_accessed=8 * terms * ROWS * SPAN,
            transcendentals=0,
        ),
    )(*operands)


def names_row():
    lane = lax.broadcasted_iota(jnp.int32, (1, 128), 1)
    return jnp.where(
        lane < NBANDS, lane, jnp.where(lane < 2 * NBANDS, lane - NBANDS, -1)
    ).astype(F32)


def band_body(y, pieces, bands, out):
    devices, each = SPAN // 36, 36
    held = bands[pl.ds(y[0] * devices, devices)].reshape(devices, each).astype(F32)
    row = lax.broadcasted_iota(jnp.int32, (SPAN, devices), 0)
    begin = lax.broadcasted_iota(jnp.int32, (SPAN, devices), 1) * each
    source = ((row >= begin) & (row < begin + each)).astype(F32)
    start = jnp.sum(source * begin.astype(F32), axis=1, keepdims=True)
    at = lax.broadcasted_iota(jnp.int32, (SPAN, each), 0).astype(F32) - start
    mask = at == lax.broadcasted_iota(jnp.int32, (SPAN, each), 1).astype(F32)
    spread = jnp.dot(source, held, preferred_element_type=F32)
    band = jnp.sum(jnp.where(mask, spread, 0.0), axis=1, keepdims=True)
    onehot = (band == names_row()).astype(F32)

    modes = jnp.sum(pieces[...], axis=0)
    sums = jnp.dot(
        (modes * modes).reshape(16, SPAN),
        onehot,
        precision=lax.Precision.HIGHEST,
        preferred_element_type=F32,
    )
    lane = lax.broadcasted_iota(jnp.int32, (8, 128), 1)
    both = jnp.where(lane < NBANDS, sums[:8], sums[8:])
    out[...] = jnp.broadcast_to(both[None], out.shape)


def final_body(blocks, bands, power, fisher):
    held = bands[...].reshape(128, 36).astype(F32).T
    label = lax.broadcasted_iota(jnp.int32, (NBANDS, 128), 0).astype(F32)
    found = jnp.zeros((NBANDS, 128), F32)
    for n in range(36):
        found += (held[n : n + 1] == label).astype(F32)
    scale = 2.0 * jnp.sum(found, axis=1, keepdims=True)
    total = jnp.sum(blocks[...].reshape(32, NY, 8, 128), axis=1).reshape(HALF, 128).T
    for c in range(2):
        for half in range(2):
            at = HALF * c + 128 * half
            power[:, at : at + 128] = (
                total[NBANDS * half : NBANDS * half + NBANDS, 128 * c : 128 * c + 128] / scale
            )
    value = power[...]
    centered = value - jnp.mean(value, axis=1, keepdims=True)
    fisher[...] = lax.dot_general(
        centered,
        centered,
        (((1,), (1,)), ((), ())),
        precision=lax.Precision.HIGHEST,
        preferred_element_type=F32,
    ) * (NMODES / NBANDS / NMAPS)


def per_device(inv_cov, sim_maps, templates, band_index):
    y = lax.axis_index("y")
    zh = lax.axis_index("zh")
    c = lax.axis_index("c")

    gathered = lax.all_gather(sim_maps, BLK, axis=0, tiled=True)

    columns = []
    for dy in range(NY):
        block = lax.dynamic_slice(templates, (0, lax.rem(y + dy, NY) * SPAN), (ROWS, SPAN))
        columns.append(lax.ppermute(block, "y", ring(dy)) if dy else block)

    bands = lax.all_to_all(
        jnp.broadcast_to(band_index[None, None, :], (128, 1, 36)), EVERY, 0, 0, tiled=True
    )
    a_high, a_low = split_rows(inv_cov)
    gathered, a_high, a_low = lax.optimization_barrier((gathered, a_high, a_low))

    got = {}
    for dy in (2, 1, 3, 0):
        if dy:
            far, near = rows_of(lax.rem(y + dy, NY), zh, a_high, a_low, gathered)
        else:
            far = block_of(2 * y + 1 - zh, a_high, a_low, gathered)
            gathered, far = lax.optimization_barrier((gathered, far))
            near = block_of(2 * y + zh, a_high, a_low, gathered)
        if dy == 2:
            far, near, bands, *columns = lax.optimization_barrier((far, near, bands, *columns))
        if dy == 3:
            far, near, *got[2] = lax.optimization_barrier((far, near, *got[2]))
        got[dy] = [shift(far, dy, 1), shift(near, dy, 0) if dy else near]
        gathered, a_high = lax.optimization_barrier((gathered, a_high, far))[:2]
    sent = [value for dy in (2, 1, 3, 0) for value in got[dy]]
    sent[-1], *columns = lax.optimization_barrier((sent[-1], *columns))
    own = jnp.stack(columns)
    *sent, own = lax.optimization_barrier((*sent, own))
    rows = sent[0]
    for value in sent[1:]:
        rows = rows + value

    keep = lax.dynamic_slice(rows, (0, c * HALF), (ROWS, HALF))
    give = lax.dynamic_slice(rows, (0, (1 - c) * HALF), (ROWS, HALF))
    pair = jnp.stack([keep, swap(give)])
    pair, own = lax.optimization_barrier((pair, own))
    other = swap(own)
    around = [shift(pair, dy, 0) if dy else pair for dy in range(NY)]
    projected = project((0,), around[:1], own, other)
    projected = project((1, 3), around[1::2], own, other, projected)
    projected = project((2,), around[2:3], own, other, projected)

    pieces = lax.all_to_all(projected, CHIPS, 0, 0, tiled=True)

    sums = pl.pallas_call(
        band_body,
        in_specs=[
            pl.BlockSpec(memory_space=pltpu.SMEM),
            pl.BlockSpec(memory_space=pltpu.VMEM),
            pl.BlockSpec(memory_space=pltpu.VMEM),
        ],
        out_shape=jax.ShapeDtypeStruct((128, 8, 128), F32),
        compiler_params=limit(32),
    )(jnp.reshape(y, (1,)).astype(jnp.int32), pieces, bands)
    blocks = lax.all_to_all(sums, ("c",) + CHIPS + ("y",), 0, 0, tiled=True)
    return pl.pallas_call(
        final_body,
        out_shape=[
            jax.ShapeDtypeStruct((NBANDS, NMAPS), F32),
            jax.ShapeDtypeStruct((NBANDS, NBANDS), F32),
        ],
        compiler_params=limit(32),
    )(blocks, bands)


def solution(mesh):
    parts = Mesh(mesh.devices.reshape(4, 2, 2, 4, 2), EVERY)
    placed = (P(BLK, RING), P(RING + BLK, None), P(BLK + RING, None), P(BLK + RING))
    body = jax.shard_map(
        per_device, mesh=parts, in_specs=placed, out_specs=(P(), P()), check_vma=False
    )
    return lambda *arrays: tuple(body(*arrays))
```

```python
import jax
import jax.numpy as jnp
from jax import lax
from jax.experimental import pallas as pl
from jax.experimental.pallas import tpu as pltpu
from jax.sharding import Mesh, PartitionSpec as P

NMODES = 4608
NBANDS = 48
NMAPS = 512
NY = 4
SPAN = NMODES // NY
HALF = NMAPS // 2
ROWS = 192
BLK = ("x", "zl", "c")
RING = ("y", "zh")
CHIPS = ("x", "zh", "zl")
EVERY = BLK + RING
MIB = 2**20
F32 = jnp.float32
BF16 = jnp.bfloat16


def split(value):
    high = value.astype(BF16)
    return high, (value - high.astype(F32)).astype(BF16)


def dot(a, b):
    return jnp.dot(a, b, preferred_element_type=F32)


def limit(mib):
    return pltpu.CompilerParams(vmem_limit_bytes=mib * MIB)


def shift(value, dy, dz):
    pairs = [
        (y * 2 + z, ((y + dy) % NY) * 2 + (z + dz) % 2)
        for y in range(NY)
        for z in range(2)
    ]
    return lax.ppermute(value, RING, pairs)


def ring(dy):
    return [(n, (n + dy) % NY) for n in range(NY)]


def swap(value):
    return lax.ppermute(value, "c", [(0, 1), (1, 0)])


def split_body(a, high, low):
    high[...], low[...] = split(a[...])


def split_rows(a):
    rows, cols = a.shape
    step = 128
    block = pl.BlockSpec((step, cols), lambda i: (i, 0))
    return pl.pallas_call(
        split_body,
        grid=(rows // step,),
        in_specs=[block],
        out_specs=[block] * 2,
        out_shape=[jax.ShapeDtypeStruct(a.shape, BF16)] * 2,
        compiler_params=limit(58),
        cost_estimate=pl.CostEstimate(
            flops=2 * rows * cols, bytes_accessed=8 * rows * cols, transcendentals=0
        ),
    )(a)


def add_step(out, value):
    @pl.when(pl.program_id(0) == 0)
    def _():
        out[...] = value

    @pl.when(pl.program_id(0) > 0)
    def _():
        out[...] += value


def row_body(at, a_high, a_low, s, far, near):
    sh, sl = split(s[...])
    ah = a_high[...]
    found = dot(ah, sh) + dot(ah, sl) + dot(a_low[...], sh)
    first, second = found[:ROWS], found[ROWS:]
    swapped = at[1] == 0
    add_step(far, jnp.where(swapped, second, first))
    add_step(near, jnp.where(swapped, first, second))


def rows_of(to, zh, a_high, a_low, maps):
    inner, cols = maps.shape
    step = 1536
    a_block = pl.BlockSpec((2 * ROWS, step), lambda k, at: (at[0], k))
    o_block = pl.BlockSpec((ROWS, cols), lambda k, at: (0, 0))
    return pl.pallas_call(
        row_body,
        grid_spec=pltpu.PrefetchScalarGridSpec(
            num_scalar_prefetch=1,
            grid=(inner // step,),
            in_specs=[a_block, a_block, pl.BlockSpec((step, cols), lambda k, at: (k, 0))],
            out_specs=[o_block] * 2,
        ),
        out_shape=[jax.ShapeDtypeStruct((ROWS, cols), F32)] * 2,
        compiler_params=limit(58),
        cost_estimate=pl.CostEstimate(
            flops=12 * ROWS * inner * cols,
            bytes_accessed=4 * inner * (2 * ROWS + cols),
            transcendentals=0,
        ),
    )(jnp.stack([to, zh]).astype(jnp.int32), a_high, a_low, maps)


def block_body(at, a_high, a_low, s, out):
    sh, sl = split(s[...])
    ah = a_high[...]
    add_step(out, dot(ah, sh) + dot(ah, sl) + dot(a_low[...], sh))


def block_of(at, a_high, a_low, maps):
    inner, cols = maps.shape
    step = 1536
    a_block = pl.BlockSpec((ROWS, step), lambda k, at: (at[0], k))
    return pl.pallas_call(
        block_body,
        grid_spec=pltpu.PrefetchScalarGridSpec(
            num_scalar_prefetch=1,
            grid=(inner // step,),
            in_specs=[a_block, a_block, pl.BlockSpec((step, cols), lambda k, at: (k, 0))],
            out_specs=pl.BlockSpec((ROWS, cols), lambda k, at: (0, 0)),
        ),
        out_shape=jax.ShapeDtypeStruct((ROWS, cols), F32),
        compiler_params=limit(58),
        cost_estimate=pl.CostEstimate(
            flops=6 * ROWS * inner * cols,
            bytes_accessed=4 * inner * (ROWS + cols),
            transcendentals=0,
        ),
    )(jnp.reshape(at, (1,)).astype(jnp.int32), a_high, a_low, maps)


def project_body(terms, begun, *refs):
    out = refs[-1]
    cols = 384
    left = []
    for t in range(terms):
        w = refs[3 * t]
        wh, wl = split(jnp.concatenate([w[0], w[1]], axis=0).T)
        left.append(jnp.concatenate([wh, wh, wl], axis=1))
    for n in range(0, SPAN, cols):
        total = None
        for t in range(terms):
            own, other = refs[3 * t + 1 : 3 * t + 3]
            th, tl = split(
                jnp.concatenate([own[0, :, n : n + cols], other[0, :, n : n + cols]], axis=0)
            )
            term = dot(left[t], jnp.concatenate([th, tl, th], axis=0))
            total = term if total is None else total + term
        for half in range(2):
            part = total[128 * half : 128 * half + 128].reshape(16, 8, cols)
            if begun:
                part += refs[3 * terms][:, half, :, n : n + cols]
            out[:, half, :, n : n + cols] = part


def project(at, weighted, own, other, begun=None):
    terms = len(weighted)
    operands = [v for w in weighted for v in (w, own, other)]
    in_specs = []
    for t in range(terms):
        block = pl.BlockSpec((1, ROWS, SPAN), lambda i, t=t: (at[t], 0, 0))
        in_specs += [pl.BlockSpec((2, ROWS, HALF), lambda i: (0, 0, 0)), block, block]
    whole = pl.BlockSpec((16, 2, 8, SPAN), lambda i: (0, 0, 0, 0))
    if begun is not None:
        operands.append(begun)
        in_specs.append(whole)

    def body(*refs):
        project_body(terms, begun is not None, *refs)

    return pl.pallas_call(
        body,
        grid=(1,),
        in_specs=in_specs,
        out_specs=whole,
        out_shape=jax.ShapeDtypeStruct((16, 2, 8, SPAN), F32),
        compiler_params=limit(32),
        cost_estimate=pl.CostEstimate(
            flops=terms * 6 * 2 * ROWS * HALF * SPAN,
            bytes_accessed=8 * terms * ROWS * SPAN,
            transcendentals=0,
        ),
    )(*operands)


def names_row():
    lane = lax.broadcasted_iota(jnp.int32, (1, 128), 1)
    return jnp.where(
        lane < NBANDS, lane, jnp.where(lane < 2 * NBANDS, lane - NBANDS, -1)
    ).astype(F32)


def band_body(y, pieces, bands, out):
    devices, each = SPAN // 36, 36
    held = bands[pl.ds(y[0] * devices, devices)].reshape(devices, each).astype(F32)
    row = lax.broadcasted_iota(jnp.int32, (SPAN, devices), 0)
    begin = lax.broadcasted_iota(jnp.int32, (SPAN, devices), 1) * each
    source = ((row >= begin) & (row < begin + each)).astype(F32)
    start = jnp.sum(source * begin.astype(F32), axis=1, keepdims=True)
    at = lax.broadcasted_iota(jnp.int32, (SPAN, each), 0).astype(F32) - start
    mask = at == lax.broadcasted_iota(jnp.int32, (SPAN, each), 1).astype(F32)
    spread = jnp.dot(source, held, preferred_element_type=F32)
    band = jnp.sum(jnp.where(mask, spread, 0.0), axis=1, keepdims=True)
    onehot = (band == names_row()).astype(F32)

    modes = jnp.sum(pieces[...], axis=0)
    sums = jnp.dot(
        (modes * modes).reshape(16, SPAN),
        onehot,
        precision=lax.Precision.HIGHEST,
        preferred_element_type=F32,
    )
    lane = lax.broadcasted_iota(jnp.int32, (8, 128), 1)
    both = jnp.where(lane < NBANDS, sums[:8], sums[8:])
    out[...] = jnp.broadcast_to(both[None], out.shape)


def final_body(blocks, bands, power, fisher):
    held = bands[...].reshape(128, 36).astype(F32).T
    label = lax.broadcasted_iota(jnp.int32, (NBANDS, 128), 0).astype(F32)
    found = jnp.zeros((NBANDS, 128), F32)
    for n in range(36):
        found += (held[n : n + 1] == label).astype(F32)
    scale = 2.0 * jnp.sum(found, axis=1, keepdims=True)
    total = jnp.sum(blocks[...].reshape(32, NY, 8, 128), axis=1).reshape(HALF, 128).T
    for c in range(2):
        for half in range(2):
            at = HALF * c + 128 * half
            power[:, at : at + 128] = (
                total[NBANDS * half : NBANDS * half + NBANDS, 128 * c : 128 * c + 128] / scale
            )
    value = power[...]
    centered = value - jnp.mean(value, axis=1, keepdims=True)
    fisher[...] = lax.dot_general(
        centered,
        centered,
        (((1,), (1,)), ((), ())),
        precision=lax.Precision.HIGHEST,
        preferred_element_type=F32,
    ) * (NMODES / NBANDS / NMAPS)


def per_device(inv_cov, sim_maps, templates, band_index):
    y = lax.axis_index("y")
    zh = lax.axis_index("zh")
    c = lax.axis_index("c")

    gathered = lax.all_gather(sim_maps, BLK, axis=0, tiled=True)

    columns = []
    for dy in range(NY):
        block = lax.dynamic_slice(templates, (0, lax.rem(y + dy, NY) * SPAN), (ROWS, SPAN))
        columns.append(lax.ppermute(block, "y", ring(dy)) if dy else block)

    bands = lax.all_to_all(
        jnp.broadcast_to(band_index[None, None, :], (128, 1, 36)), EVERY, 0, 0, tiled=True
    )
    a_high, a_low = split_rows(inv_cov)
    gathered, a_high, a_low = lax.optimization_barrier((gathered, a_high, a_low))

    got = {}
    for dy in (1, 3, 2, 0):
        if dy:
            far, near = rows_of(lax.rem(y + dy, NY), zh, a_high, a_low, gathered)
        else:
            far = block_of(2 * y + 1 - zh, a_high, a_low, gathered)
            gathered, far = lax.optimization_barrier((gathered, far))
            near = block_of(2 * y + zh, a_high, a_low, gathered)
        if dy == 1:
            far, near, bands, *columns = lax.optimization_barrier((far, near, bands, *columns))
        if dy == 2:
            far, near, *got[1] = lax.optimization_barrier((far, near, *got[1]))
        got[dy] = [shift(far, dy, 1), shift(near, dy, 0) if dy else near]
        gathered, a_high = lax.optimization_barrier((gathered, a_high, far))[:2]
    sent = [value for dy in (1, 3, 2, 0) for value in got[dy]]
    sent[-1], *columns = lax.optimization_barrier((sent[-1], *columns))
    own = jnp.stack(columns)
    *sent, own = lax.optimization_barrier((*sent, own))
    rows = sent[0]
    for value in sent[1:]:
        rows = rows + value

    keep = lax.dynamic_slice(rows, (0, c * HALF), (ROWS, HALF))
    give = lax.dynamic_slice(rows, (0, (1 - c) * HALF), (ROWS, HALF))
    pair = jnp.stack([keep, swap(give)])
    pair, own = lax.optimization_barrier((pair, own))
    other = swap(own)
    around = [shift(pair, dy, 0) if dy else pair for dy in range(NY)]
    projected = project((0,), around[:1], own, other)
    projected = project((1, 3), around[1::2], own, other, projected)
    projected = project((2,), around[2:3], own, other, projected)

    pieces = lax.all_to_all(projected, CHIPS, 0, 0, tiled=True)

    sums = pl.pallas_call(
        band_body,
        in_specs=[
            pl.BlockSpec(memory_space=pltpu.SMEM),
            pl.BlockSpec(memory_space=pltpu.VMEM),
            pl.BlockSpec(memory_space=pltpu.VMEM),
        ],
        out_shape=jax.ShapeDtypeStruct((128, 8, 128), F32),
        compiler_params=limit(32),
    )(jnp.reshape(y, (1,)).astype(jnp.int32), pieces, bands)
    blocks = lax.all_to_all(sums, ("c",) + CHIPS + ("y",), 0, 0, tiled=True)
    return pl.pallas_call(
        final_body,
        out_shape=[
            jax.ShapeDtypeStruct((NBANDS, NMAPS), F32),
            jax.ShapeDtypeStruct((NBANDS, NBANDS), F32),
        ],
        compiler_params=limit(32),
    )(blocks, bands)


def solution(mesh):
    parts = Mesh(mesh.devices.reshape(4, 2, 2, 4, 2), EVERY)
    placed = (P(BLK, RING), P(RING + BLK, None), P(BLK + RING, None), P(BLK + RING))
    body = jax.shard_map(
        per_device, mesh=parts, in_specs=placed, out_specs=(P(), P()), check_vma=False
    )
    return lambda *arrays: tuple(body(*arrays))
```

```python
import jax
import jax.numpy as jnp
from jax import lax
from jax.experimental import pallas as pl
from jax.experimental.pallas import tpu as pltpu
from jax.sharding import Mesh, PartitionSpec as P

NMODES = 4608
NBANDS = 48
NMAPS = 512
NY = 4
SPAN = NMODES // NY
HALF = NMAPS // 2
ROWS = 192
BLK = ("x", "zl", "c")
RING = ("y", "zh")
CHIPS = ("x", "zh", "zl")
EVERY = BLK + RING
MIB = 2**20
F32 = jnp.float32
BF16 = jnp.bfloat16


def split(value):
    high = value.astype(BF16)
    return high, (value - high.astype(F32)).astype(BF16)


def dot(a, b):
    return jnp.dot(a, b, preferred_element_type=F32)


def limit(mib):
    return pltpu.CompilerParams(vmem_limit_bytes=mib * MIB)


def shift(value, dy, dz):
    pairs = [
        (y * 2 + z, ((y + dy) % NY) * 2 + (z + dz) % 2)
        for y in range(NY)
        for z in range(2)
    ]
    return lax.ppermute(value, RING, pairs)


def ring(dy):
    return [(n, (n + dy) % NY) for n in range(NY)]


def swap(value):
    return lax.ppermute(value, "c", [(0, 1), (1, 0)])


def split_body(a, high, low):
    high[...], low[...] = split(a[...])


def split_rows(a):
    rows, cols = a.shape
    step = 128
    block = pl.BlockSpec((step, cols), lambda i: (i, 0))
    return pl.pallas_call(
        split_body,
        grid=(rows // step,),
        in_specs=[block],
        out_specs=[block] * 2,
        out_shape=[jax.ShapeDtypeStruct(a.shape, BF16)] * 2,
        compiler_params=limit(58),
        cost_estimate=pl.CostEstimate(
            flops=2 * rows * cols, bytes_accessed=8 * rows * cols, transcendentals=0
        ),
    )(a)


def add_step(out, value):
    @pl.when(pl.program_id(0) == 0)
    def _():
        out[...] = value

    @pl.when(pl.program_id(0) > 0)
    def _():
        out[...] += value


def row_body(at, a_high, a_low, s, far, near):
    sh, sl = split(s[...])
    ah = a_high[...]
    found = dot(ah, sh) + dot(ah, sl) + dot(a_low[...], sh)
    first, second = found[:ROWS], found[ROWS:]
    swapped = at[1] == 0
    add_step(far, jnp.where(swapped, second, first))
    add_step(near, jnp.where(swapped, first, second))


def rows_of(to, zh, a_high, a_low, maps):
    inner, cols = maps.shape
    step = 1536
    a_block = pl.BlockSpec((2 * ROWS, step), lambda k, at: (at[0], k))
    o_block = pl.BlockSpec((ROWS, cols), lambda k, at: (0, 0))
    return pl.pallas_call(
        row_body,
        grid_spec=pltpu.PrefetchScalarGridSpec(
            num_scalar_prefetch=1,
            grid=(inner // step,),
            in_specs=[a_block, a_block, pl.BlockSpec((step, cols), lambda k, at: (k, 0))],
            out_specs=[o_block] * 2,
        ),
        out_shape=[jax.ShapeDtypeStruct((ROWS, cols), F32)] * 2,
        compiler_params=limit(58),
        cost_estimate=pl.CostEstimate(
            flops=12 * ROWS * inner * cols,
            bytes_accessed=4 * inner * (2 * ROWS + cols),
            transcendentals=0,
        ),
    )(jnp.stack([to, zh]).astype(jnp.int32), a_high, a_low, maps)


def block_body(at, a_high, a_low, s, out):
    sh, sl = split(s[...])
    ah = a_high[...]
    add_step(out, dot(ah, sh) + dot(ah, sl) + dot(a_low[...], sh))


def block_of(at, a_high, a_low, maps):
    inner, cols = maps.shape
    step = 1536
    a_block = pl.BlockSpec((ROWS, step), lambda k, at: (at[0], k))
    return pl.pallas_call(
        block_body,
        grid_spec=pltpu.PrefetchScalarGridSpec(
            num_scalar_prefetch=1,
            grid=(inner // step,),
            in_specs=[a_block, a_block, pl.BlockSpec((step, cols), lambda k, at: (k, 0))],
            out_specs=pl.BlockSpec((ROWS, cols), lambda k, at: (0, 0)),
        ),
        out_shape=jax.ShapeDtypeStruct((ROWS, cols), F32),
        compiler_params=limit(58),
        cost_estimate=pl.CostEstimate(
            flops=6 * ROWS * inner * cols,
            bytes_accessed=4 * inner * (ROWS + cols),
            transcendentals=0,
        ),
    )(jnp.reshape(at, (1,)).astype(jnp.int32), a_high, a_low, maps)


def project_body(terms, begun, *refs):
    out = refs[-1]
    cols = 384
    left = []
    for t in range(terms):
        w = refs[3 * t]
        wh, wl = split(jnp.concatenate([w[0], w[1]], axis=0).T)
        left.append(jnp.concatenate([wh, wh, wl], axis=1))
    for n in range(0, SPAN, cols):
        total = None
        for t in range(terms):
            own, other = refs[3 * t + 1 : 3 * t + 3]
            th, tl = split(
                jnp.concatenate([own[0, :, n : n + cols], other[0, :, n : n + cols]], axis=0)
            )
            term = dot(left[t], jnp.concatenate([th, tl, th], axis=0))
            total = term if total is None else total + term
        for half in range(2):
            part = total[128 * half : 128 * half + 128].reshape(16, 8, cols)
            if begun:
                part += refs[3 * terms][:, half, :, n : n + cols]
            out[:, half, :, n : n + cols] = part


def project(at, weighted, own, other, begun=None):
    terms = len(weighted)
    operands = [v for w in weighted for v in (w, own, other)]
    in_specs = []
    for t in range(terms):
        block = pl.BlockSpec((1, ROWS, SPAN), lambda i, t=t: (at[t], 0, 0))
        in_specs += [pl.BlockSpec((2, ROWS, HALF), lambda i: (0, 0, 0)), block, block]
    whole = pl.BlockSpec((16, 2, 8, SPAN), lambda i: (0, 0, 0, 0))
    if begun is not None:
        operands.append(begun)
        in_specs.append(whole)

    def body(*refs):
        project_body(terms, begun is not None, *refs)

    return pl.pallas_call(
        body,
        grid=(1,),
        in_specs=in_specs,
        out_specs=whole,
        out_shape=jax.ShapeDtypeStruct((16, 2, 8, SPAN), F32),
        compiler_params=limit(32),
        cost_estimate=pl.CostEstimate(
            flops=terms * 6 * 2 * ROWS * HALF * SPAN,
            bytes_accessed=8 * terms * ROWS * SPAN,
            transcendentals=0,
        ),
    )(*operands)


def names_row():
    lane = lax.broadcasted_iota(jnp.int32, (1, 128), 1)
    return jnp.where(
        lane < NBANDS, lane, jnp.where(lane < 2 * NBANDS, lane - NBANDS, -1)
    ).astype(F32)


def band_body(y, pieces, bands, out):
    devices, each = SPAN // 36, 36
    held = bands[pl.ds(y[0] * devices, devices)].reshape(devices, each).astype(F32)
    row = lax.broadcasted_iota(jnp.int32, (SPAN, devices), 0)
    begin = lax.broadcasted_iota(jnp.int32, (SPAN, devices), 1) * each
    source = ((row >= begin) & (row < begin + each)).astype(F32)
    start = jnp.sum(source * begin.astype(F32), axis=1, keepdims=True)
    at = lax.broadcasted_iota(jnp.int32, (SPAN, each), 0).astype(F32) - start
    mask = at == lax.broadcasted_iota(jnp.int32, (SPAN, each), 1).astype(F32)
    spread = jnp.dot(source, held, preferred_element_type=F32)
    band = jnp.sum(jnp.where(mask, spread, 0.0), axis=1, keepdims=True)
    onehot = (band == names_row()).astype(F32)

    modes = jnp.sum(pieces[...], axis=0)
    sums = jnp.dot(
        (modes * modes).reshape(16, SPAN),
        onehot,
        precision=lax.Precision.HIGHEST,
        preferred_element_type=F32,
    )
    lane = lax.broadcasted_iota(jnp.int32, (8, 128), 1)
    both = jnp.where(lane < NBANDS, sums[:8], sums[8:])
    out[...] = jnp.broadcast_to(both[None], out.shape)


def final_body(blocks, bands, power, fisher):
    held = bands[...].reshape(128, 36).astype(F32).T
    label = lax.broadcasted_iota(jnp.int32, (NBANDS, 128), 0).astype(F32)
    found = jnp.zeros((NBANDS, 128), F32)
    for n in range(36):
        found += (held[n : n + 1] == label).astype(F32)
    scale = 2.0 * jnp.sum(found, axis=1, keepdims=True)
    total = jnp.sum(blocks[...].reshape(32, NY, 8, 128), axis=1).reshape(HALF, 128).T
    for c in range(2):
        for half in range(2):
            at = HALF * c + 128 * half
            power[:, at : at + 128] = (
                total[NBANDS * half : NBANDS * half + NBANDS, 128 * c : 128 * c + 128] / scale
            )
    value = power[...]
    centered = value - jnp.mean(value, axis=1, keepdims=True)
    fisher[...] = lax.dot_general(
        centered,
        centered,
        (((1,), (1,)), ((), ())),
        precision=lax.Precision.HIGHEST,
        preferred_element_type=F32,
    ) * (NMODES / NBANDS / NMAPS)


def per_device(inv_cov, sim_maps, templates, band_index):
    y = lax.axis_index("y")
    zh = lax.axis_index("zh")
    c = lax.axis_index("c")

    gathered = lax.all_gather(sim_maps, BLK, axis=0, tiled=True)

    columns = []
    for dy in range(NY):
        block = lax.dynamic_slice(templates, (0, lax.rem(y + dy, NY) * SPAN), (ROWS, SPAN))
        columns.append(lax.ppermute(block, "y", ring(dy)) if dy else block)

    bands = lax.all_to_all(
        jnp.broadcast_to(band_index[None, None, :], (128, 1, 36)), EVERY, 0, 0, tiled=True
    )
    a_high, a_low = split_rows(inv_cov)
    gathered, a_high, a_low = lax.optimization_barrier((gathered, a_high, a_low))

    got = {}
    for dy in (2, 1, 3, 0):
        to = lax.rem(y + dy, NY)
        if dy % 2:
            far, near = rows_of(to, zh, a_high, a_low, gathered)
        else:
            far = block_of(2 * to + 1 - zh, a_high, a_low, gathered)
            gathered, far = lax.optimization_barrier((gathered, far))
            near = block_of(2 * to + zh, a_high, a_low, gathered)
        if dy == 2:
            far, near, bands, *columns = lax.optimization_barrier((far, near, bands, *columns))
        if dy == 3:
            far, near, *got[2] = lax.optimization_barrier((far, near, *got[2]))
        got[dy] = [shift(far, dy, 1), shift(near, dy, 0) if dy else near]
        gathered, a_high = lax.optimization_barrier((gathered, a_high, far))[:2]
    sent = [value for dy in (2, 1, 3, 0) for value in got[dy]]
    sent[-1], *columns = lax.optimization_barrier((sent[-1], *columns))
    own = jnp.stack(columns)
    *sent, own = lax.optimization_barrier((*sent, own))
    rows = sent[0]
    for value in sent[1:]:
        rows = rows + value

    keep = lax.dynamic_slice(rows, (0, c * HALF), (ROWS, HALF))
    give = lax.dynamic_slice(rows, (0, (1 - c) * HALF), (ROWS, HALF))
    pair = jnp.stack([keep, swap(give)])
    pair, own = lax.optimization_barrier((pair, own))
    other = swap(own)
    around = [shift(pair, dy, 0) if dy else pair for dy in range(NY)]
    projected = project((0,), around[:1], own, other)
    projected = project((1, 3), around[1::2], own, other, projected)
    projected = project((2,), around[2:3], own, other, projected)

    pieces = lax.all_to_all(projected, CHIPS, 0, 0, tiled=True)

    sums = pl.pallas_call(
        band_body,
        in_specs=[
            pl.BlockSpec(memory_space=pltpu.SMEM),
            pl.BlockSpec(memory_space=pltpu.VMEM),
            pl.BlockSpec(memory_space=pltpu.VMEM),
        ],
        out_shape=jax.ShapeDtypeStruct((128, 8, 128), F32),
        compiler_params=limit(32),
    )(jnp.reshape(y, (1,)).astype(jnp.int32), pieces, bands)
    blocks = lax.all_to_all(sums, ("c",) + CHIPS + ("y",), 0, 0, tiled=True)
    return pl.pallas_call(
        final_body,
        out_shape=[
            jax.ShapeDtypeStruct((NBANDS, NMAPS), F32),
            jax.ShapeDtypeStruct((NBANDS, NBANDS), F32),
        ],
        compiler_params=limit(32),
    )(blocks, bands)


def solution(mesh):
    parts = Mesh(mesh.devices.reshape(4, 2, 2, 4, 2), EVERY)
    placed = (P(BLK, RING), P(RING + BLK, None), P(BLK + RING, None), P(BLK + RING))
    body = jax.shard_map(
        per_device, mesh=parts, in_specs=placed, out_specs=(P(), P()), check_vma=False
    )
    return lambda *arrays: tuple(body(*arrays))
```
